256 devices in a mesh: pipe: 2 (over y_hi), expert: 8 (over z), tensor: 16 (over x, y_lo, core).
Axes of the slice: x: 4, y: 4 (y_hi: 2, y_lo: 2; y = y_hi * 2 + y_lo), z: 8, core: 2. Of those that a mesh axis runs over, the one named last changes fastest.
Arguments:
- stream: bfloat16 [2048, 6144], P(('pipe', 'expert'), 'tensor')
- norm_gain: float32 [6144], P('tensor'), may hold values from 0.5 to 1.5
- attn_gain: float32 [6144], P('tensor'), may hold values from 0.5 to 1.5
- router: float32 [6144, 8], P('tensor'), may hold values from -0.078125 to 0.078125
- expert_ids: int32 [2048, 2], P(('pipe', 'expert')), may hold values from 0 to 7, as said below
- expert_slots: int32 [2048, 2], P(('pipe', 'expert')), may hold values from -1 to 39, as said below
- w_gate: bfloat16 [8, 6144, 8192], P('expert', None, ('pipe', 'tensor')), may hold values from -0.078125 to 0.078125
- w_up: bfloat16 [8, 6144, 8192], P('expert', None, ('pipe', 'tensor')), may hold values from -0.078125 to 0.078125
- w_down: bfloat16 [8, 8192, 6144], P('expert', ('pipe', 'tensor')), may hold values from -0.125 to 0.125
- w_query: bfloat16 [6144, 6144], P('tensor', ('pipe', 'expert'))
- w_key: bfloat16 [6144, 1024], P('tensor')
- w_value: bfloat16 [6144, 1024], P('tensor'), may hold values from -0.078125 to 0.078125
Outputs:
- new_stream: bfloat16 [2048, 6144], P(('pipe', 'expert'), 'tensor')
- attended: bfloat16 [2048, 6144], P('tensor', ('pipe', 'expert'))
The draws below stay inside these ranges and needn't reach their ends.
Inputs may be any that keep to these rules, and one draw needn't show every extreme that they name: `expert_ids`: each row names two different experts. `expert_slots`: within the rows of one group of 128 tokens, each expert's picks take slots 0, 1, 2 and so on in token order (pick 0 before pick 1) until 40 are taken, later picks of that expert are -1; so each pair of expert and slot is named at most once in a group.
All inputs are finite; a program needn't handle non-finite values.
Results may differ from the reference program's by a relative error of at most 0.015.
Values may be sent and summed in bfloat16 or wider, within the bound.
No kernel may reach another device: no remote copies, remote signals or barrier semaphores. Data moves between devices by JAX's collectives and lax.ppermute only.
A program may use at most 128 MiB of HBM per device.

```python
import math
import jax
import jax.numpy as jnp
from jax import lax

D = 6144
FF = 8192
QH = 48
KVH = 8
HD = 128
TOK_DEV = 128
EXPERTS = 8
TOKENS = 2048
CAP = 40
N_PIPE = 2
N_EXPERT = 8


def routing(base_key):
    key_base, key_global, key_block = jax.random.split(base_key, 3)
    groups = TOKENS // TOK_DEV
    noise = jax.random.randint(key_base, (TOKENS, EXPERTS), 0, 64)
    favour = jax.random.permutation(key_global, EXPERTS) * 4
    block_keys = jax.random.split(key_block, groups)
    local_bias = jax.vmap(lambda single: jax.random.permutation(single, EXPERTS))(block_keys) * 2
    scores = noise + favour[None, :] + jnp.repeat(local_bias, TOK_DEV, axis=0)
    distinct = scores * EXPERTS + jnp.arange(EXPERTS, dtype=jnp.int32)[None, :]
    picks = lax.top_k(distinct, 2)[1].astype(jnp.int32)
    marks = (picks[:, :, None] == jnp.arange(EXPERTS, dtype=jnp.int32)[None, None, :]).astype(jnp.int32)
    marks = marks.reshape(groups, TOK_DEV * 2, EXPERTS)
    ranks = jnp.cumsum(marks, axis=1) - marks
    slot_rank = jnp.sum(ranks * marks, axis=2).reshape(TOKENS, 2)
    slots = jnp.where(slot_rank < CAP, slot_rank, -1).astype(jnp.int32)
    return (picks, slots)


def key_matrix(base_key):
    return jax.random.normal(jax.random.fold_in(base_key, 5), (D, KVH * HD), jnp.float32) * D ** (-0.5)


def draw_expert_ids(key, part):
    picks, slots = routing(key)
    return picks


def draw_expert_slots(key, part):
    picks, slots = routing(key)
    return slots


def draw_w_key(key, part):
    shared = key_matrix(key)
    return shared.astype(jnp.bfloat16)


def draw_w_query(key, part):
    key = jax.random.fold_in(key, 43)
    key_drawn = jax.random.fold_in(key, 0)
    drawn = jax.random.normal(key_drawn, (D, QH * HD), jnp.float32) * D ** (-0.5)
    return drawn.astype(jnp.bfloat16)


def draw_stream(key, part):
    key = jax.random.fold_in(key, 11)
    key_values, key_rows = jax.random.split(key)
    column = jnp.arange(D, dtype=jnp.float32) / D
    values = jax.random.normal(key_values, (TOKENS, D), jnp.float32)
    column_scale = 10.0 ** column
    row_scale = jnp.exp(jax.random.uniform(key_rows, (TOKENS, 1), jnp.float32, 0.0, math.log(10.0)))
    return (values * column_scale[None, :] * row_scale * 0.15).astype(jnp.bfloat16)


def with_spikes(values, key, source, target, shards_of, factor):
    def block_of(position):
        return (jnp.arange(values.shape[position]) // (values.shape[position] // shards_of)).reshape((-1,) + (1,) * (values.ndim - 1 - position))

    near = jax.random.permutation(key, shards_of)[block_of(target)]
    other_side = (block_of(target) + shards_of // 2) % shards_of
    return jnp.where((block_of(source) == near) | (block_of(source) == other_side), factor * values, values)


def shard_levels(own_key, dims, cuts, least, largest):
    loudness, own = 1.0, jax.random.fold_in(own_key, 6)
    for dim, shards_of in cuts:
        heights = jnp.exp(jax.random.uniform(jax.random.fold_in(own, dim), (shards_of,), jnp.float32, least / len(cuts), largest / len(cuts)))
        loudness = loudness * jnp.repeat(heights, dims[dim] // shards_of).reshape([-1 if axis == dim else 1 for axis in range(len(dims))])
    return loudness


def normal_values(rng, shape, spread, bound, shards=(), kind=jnp.bfloat16):
    array = jax.random.normal(rng, shape, jnp.float32) * spread
    if len(shards) > 0:
        array = shard_levels(rng, shape, shards, -0.22, 0.18) * array
    return jnp.clip(array, min=-bound, max=bound).astype(kind)


def bell_draw_with(key, extent, width, most, cuts, heavy, kind=jnp.bfloat16):
    array = width * jax.random.normal(key, extent, jnp.float32)
    if cuts:
        array = array * shard_levels(key, extent, cuts, -0.22, 0.18)
    return jnp.clip(with_spikes(array, jax.random.fold_in(key, 3), *heavy), -most, most).astype(kind)


def setup_inputs(seed: int = 0) -> dict:
    arg_keys = jax.random.split(jax.random.key(seed), 13)
    stream = draw_stream(jax.random.fold_in(arg_keys[12], 71), 0)
    norm_gain = jnp.clip(1.0 + 0.1 * jax.random.normal(arg_keys[1], (D,), jnp.float32), 0.5, 1.5)
    attn_gain = jnp.clip(1.0 + 0.1 * jax.random.normal(arg_keys[2], (D,), jnp.float32), 0.5, 1.5)
    router = normal_values(arg_keys[3], (D, EXPERTS), D ** -0.5, 0.078125, ((0, 16),), jnp.float32)
    expert_ids = draw_expert_ids(jax.random.fold_in(arg_keys[12], 71), 0)
    expert_slots = draw_expert_slots(jax.random.fold_in(arg_keys[12], 71), 0)
    w_gate = normal_values(arg_keys[6], (EXPERTS, D, FF), D ** -0.5, 0.078125, ((0, 8), (2, 32)))
    w_up = normal_values(arg_keys[7], (EXPERTS, D, FF), D ** -0.5, 0.078125, ((0, 8), (2, 32)))
    w_down = bell_draw_with(arg_keys[8], (EXPERTS, FF, D), FF ** -0.5, 0.125, ((0, 8), (1, 32)), (1, 2, 32, 2.75))
    w_query = draw_w_query(jax.random.fold_in(arg_keys[12], 71), 0)
    w_key = draw_w_key(jax.random.fold_in(arg_keys[12], 71), 0)
    w_value = normal_values(arg_keys[11], (D, KVH * HD), D ** -0.5, 0.078125, ((0, 16),))
    return {"stream": stream, "norm_gain": norm_gain, "attn_gain": attn_gain, "router": router, "expert_ids": expert_ids, "expert_slots": expert_slots, "w_gate": w_gate, "w_up": w_up, "w_down": w_down, "w_query": w_query, "w_key": w_key, "w_value": w_value}


NORM_EPS = 1e-05

def expert_apply(operands):
    buffer_rows, gate_weight, up_weight, down_weight = operands
    gate_value = jnp.dot(buffer_rows, gate_weight, preferred_element_type=jnp.float32)
    up_value = jnp.dot(buffer_rows, up_weight, preferred_element_type=jnp.float32)
    hidden_value = (jax.nn.silu(gate_value) * up_value).astype(jnp.bfloat16)
    return jnp.dot(hidden_value, down_weight, preferred_element_type=jnp.float32).astype(jnp.bfloat16)

def head_attend(operands):
    query_head, key_head, value_head = operands
    scores = jnp.dot(query_head, key_head.T, preferred_element_type=jnp.float32) * (1.0 / math.sqrt(HD))
    positions = jnp.arange(query_head.shape[0], dtype=jnp.int32)
    allowed = positions[None, :] <= positions[:, None]
    masked = jnp.where(allowed, scores, -1e+30)
    highest = lax.optimization_barrier(jnp.max(masked, axis=1, keepdims=True))
    weights = jnp.where(allowed, jnp.exp(masked - highest), 0.0)
    totals = lax.optimization_barrier(jnp.sum(weights, axis=1, keepdims=True))
    return jnp.dot(weights.astype(jnp.bfloat16), value_head, preferred_element_type=jnp.float32) / totals

def reference(stream, norm_gain, attn_gain, router, expert_ids, expert_slots, w_gate, w_up, w_down, w_query, w_key, w_value):
    groups = N_PIPE * N_EXPERT
    stream_f = stream.astype(jnp.float32)
    squares = lax.optimization_barrier(jnp.sum(stream_f * stream_f, axis=1))
    inverse = lax.rsqrt(squares / D + NORM_EPS)
    scaled = stream_f * norm_gain
    normed = (scaled * inverse[:, None]).astype(jnp.bfloat16)
    logits = inverse[:, None] * jnp.dot(scaled, router, precision=lax.Precision.HIGHEST)
    onehot = expert_ids[:, :, None] == jnp.arange(EXPERTS, dtype=jnp.int32)[None, None, :]
    picked = lax.optimization_barrier(jnp.sum(jnp.where(onehot, logits[:, None, :], 0.0), axis=2))
    first_share = jax.nn.sigmoid(picked[:, 0] - picked[:, 1])
    mixing = jnp.stack([first_share, 1.0 - first_share], axis=1)
    owner = jnp.arange(TOKENS, dtype=jnp.int32) // TOK_DEV
    slot_total = groups * EXPERTS * CAP
    target = jnp.where(expert_slots >= 0, (owner[:, None] * EXPERTS + expert_ids) * CAP + expert_slots, slot_total).astype(jnp.int32)
    copies = jnp.broadcast_to(normed[:, None, :], (TOKENS, 2, D)).reshape(TOKENS * 2, D)
    buffer = jnp.zeros((slot_total + 1, D), jnp.bfloat16).at[target.reshape(-1)].set(copies)[:slot_total]
    by_expert = buffer.reshape(groups, EXPERTS, CAP, D).transpose(1, 0, 2, 3).reshape(EXPERTS, groups * CAP, D)
    produced = lax.map(expert_apply, (by_expert, w_gate, w_up, w_down))
    returned = produced.reshape(EXPERTS, groups, CAP, D).transpose(1, 0, 2, 3).reshape(slot_total, D)
    padded = jnp.concatenate([returned, jnp.zeros((1, D), jnp.bfloat16)], axis=0)
    gathered = padded[target].astype(jnp.float32)
    moe_sum = lax.optimization_barrier(jnp.sum(mixing[:, :, None] * gathered, axis=1))
    new_stream = (stream_f + moe_sum).astype(jnp.bfloat16)
    attn_f = new_stream.astype(jnp.float32)
    inverse_two = lax.rsqrt(lax.optimization_barrier(jnp.sum(attn_f * attn_f, axis=1)) / D + NORM_EPS)
    attn_in = (attn_f * inverse_two[:, None] * attn_gain).astype(jnp.bfloat16)
    queries = jnp.dot(attn_in, w_query, preferred_element_type=jnp.float32).astype(jnp.bfloat16)
    queries = queries.reshape(TOKENS, QH, HD).transpose(1, 0, 2)
    key_rows = jnp.dot(attn_in, w_key, preferred_element_type=jnp.float32).astype(jnp.bfloat16)
    key_rows = key_rows.reshape(TOKENS, KVH, HD).transpose(1, 0, 2)
    value_rows = jnp.dot(attn_in, w_value, preferred_element_type=jnp.float32).astype(jnp.bfloat16)
    value_rows = value_rows.reshape(TOKENS, KVH, HD).transpose(1, 0, 2)
    sharing = jnp.arange(QH, dtype=jnp.int32) // (QH // KVH)
    contexts = lax.map(head_attend, (queries, key_rows[sharing], value_rows[sharing]))
    attended = contexts.transpose(1, 0, 2).reshape(TOKENS, QH * HD).astype(jnp.bfloat16)
    return (new_stream, attended)
```

```python
import functools
import math

import jax
import jax.numpy as jnp
from jax import lax
from jax.experimental import pallas as pl
from jax.experimental.pallas import tpu as pltpu
from jax.sharding import PartitionSpec as P

HD = 128
QH = 48
KVH = 8
CAP = 40
NORM_EPS = 1e-05
N_TENSOR = 16
BF = jnp.bfloat16
F32 = jnp.float32
VMEM_BYTES = 40 * 1024 * 1024


def from_plane(value, dx, dy):
    pairs = []
    for x in range(4):
        for yy in range(4):
            for core in range(2):
                source = (yy // 2) * 16 + x * 4 + (yy % 2) * 2 + core
                tx, ty = (x - dx) % 4, (yy - dy) % 4
                pairs.append((source, (ty // 2) * 16 + tx * 4 + (ty % 2) * 2 + core))
    return lax.ppermute(value, ("pipe", "tensor"), pairs)


def from_x(value, dx):
    pairs = [(i, (i - 4 * dx) % 16) for i in range(16)]
    return lax.ppermute(value, "tensor", pairs)


def from_flip(value, bit):
    return lax.ppermute(value, "tensor", [(i, i ^ bit) for i in range(16)])


def from_z(value, dz):
    return lax.ppermute(value, "expert", [(i, (i - dz) % 8) for i in range(8)])


def from_pipe(value):
    return lax.ppermute(value, "pipe", [(0, 1), (1, 0)])


def place(scal):
    t = scal[0]
    yy = scal[1]
    return lax.shift_right_logical(t, 2), yy, lax.bitwise_and(t, 1)


def plane_target(scal, dc, dy, dx):
    x, yy, core = place(scal)
    tx = lax.bitwise_and(x + dx, 3)
    ty = lax.bitwise_and(yy + dy, 3)
    pipe = lax.shift_right_logical(ty, 1)
    tensor = tx * 4 + lax.bitwise_and(ty, 1) * 2 + lax.bitwise_xor(core, dc)
    return pipe, tensor


def sigmoid(v):
    return 1.0 / (1.0 + jnp.exp(-v))


X_NAMES = ("xa", "au", "ad", "ah0", "ah1", "yb", "bu", "bd", "bh0", "bh1")


def a_piece(dy, dx):
    if dy == 0:
        return "xa", dx
    if dy == 1:
        return "au", dx
    if dy == 3:
        return "ad", dx
    return ("ah0", dx) if dx < 2 else ("ah1", dx - 2)


def b_piece(dy, dx):
    if dx == 0:
        return "yb", dy
    if dx == 1:
        return "bu", dy
    if dx == 3:
        return "bd", dy
    return ("bh0", dy) if dy < 2 else ("bh1", dy - 2)


def gate_up_kernel(width, *refs):
    scal, gains = refs[0], refs[1]
    near = dict(zip(X_NAMES, refs[2:12]))
    far = dict(zip(X_NAMES, refs[12:22]))
    wg, wu, hidden, xbuf, gbuf, ubuf, acc, ssq, xsem, wsem = refs[22:]
    half = xbuf.shape[1] // 2
    order = [(dc, dy, dx) for dc in range(2) for dy in (0, 1, 3, 2) for dx in range(4)]
    x_copies, w_copies = [], {}
    for i, (dc, dy, dx) in enumerate(order):
        w = dc * 8 + (dy & 1) * 4 + dx
        if w not in w_copies:
            _, t = plane_target(scal, dc, dy, dx)
            rows = pl.ds(pl.multiple_of(t * width, 128), width)
            pair = (
                pltpu.make_async_copy(wg.at[rows, :], gbuf.at[w], wsem.at[w, 0]),
                pltpu.make_async_copy(wu.at[rows, :], ubuf.at[w], wsem.at[w, 1]),
            )
            for copy in pair:
                copy.start()
            w_copies[w] = pair
        table = far if dc else near
        name_a, at_a = a_piece(dy, dx)
        name_b, at_b = b_piece(dy, dx)
        pair = (
            pltpu.make_async_copy(
                table[name_a].at[at_a], xbuf.at[i, pl.ds(0, half), :], xsem.at[i, 0]
            ),
            pltpu.make_async_copy(
                table[name_b].at[at_b], xbuf.at[i, pl.ds(half, half), :], xsem.at[i, 1]
            ),
        )
        for copy in pair:
            copy.start()
        x_copies.append(pair)
    acc[...] = jnp.zeros_like(acc)
    ssq[...] = jnp.zeros_like(ssq)
    own = scal[0]
    waited = set()
    columns = wg.shape[1]
    for i, (dc, dy, dx) in enumerate(order):
        w = dc * 8 + (dy & 1) * 4 + dx
        if w not in waited:
            waited.add(w)
            for copy in w_copies[w]:
                copy.wait()
        for copy in x_copies[i]:
            copy.wait()
        pipe, t = plane_target(scal, dc, dy, dx)
        rows = xbuf[i].astype(F32)
        squares = rows * rows
        part = squares[:, 0:128]
        for j in range(1, width // 128):
            part = part + squares[:, j * 128 : (j + 1) * 128]
        ssq[pipe] += part
        left = (rows * gains[lax.bitwise_xor(t, own)]).astype(BF)
        acc[pipe, :, 0:columns] += jnp.dot(left, gbuf[w], preferred_element_type=F32)
        acc[pipe, :, columns:] += jnp.dot(left, ubuf[w], preferred_element_type=F32)
    for pipe in range(2):
        total = jnp.sum(ssq[pipe], axis=1, keepdims=True)
        inverse = lax.rsqrt(total / (width * N_TENSOR) + NORM_EPS)
        keep = inverse > 0.0
        gate = jnp.where(keep, acc[pipe, :, 0:columns] * inverse, 0.0)
        up = jnp.where(keep, acc[pipe, :, columns:] * inverse, 0.0)
        hidden[pipe] = (gate * sigmoid(gate) * up).astype(BF)


ANY = pl.BlockSpec(memory_space=pl.ANY)
IN_VMEM = pl.BlockSpec(memory_space=pltpu.VMEM)
IN_SMEM = pl.BlockSpec(memory_space=pltpu.SMEM)


def params():
    return pltpu.CompilerParams(vmem_limit_bytes=VMEM_BYTES)


def gate_up(scal, gains, near, far, wg, wu):
    width = near[0].shape[-1]
    rows = near[0].shape[1] * 2
    columns = wg.shape[1]
    return pl.pallas_call(
        functools.partial(gate_up_kernel, width),
        out_shape=jax.ShapeDtypeStruct((2, rows, columns), BF),
        in_specs=[IN_SMEM, IN_VMEM] + [ANY] * 22,
        out_specs=IN_VMEM,
        scratch_shapes=[
            pltpu.VMEM((32, rows, width), BF),
            pltpu.VMEM((16, width, columns), BF),
            pltpu.VMEM((16, width, columns), BF),
            pltpu.VMEM((2, rows, 2 * columns), F32),
            pltpu.VMEM((2, rows, 128), F32),
            pltpu.SemaphoreType.DMA((32, 2)),
            pltpu.SemaphoreType.DMA((16, 2)),
        ],
        compiler_params=params(),
        name="gate_up",
    )(scal, gains, *near, *far, wg, wu)


FIRST, LATER = 0, {0: 0, 1: 4, 3: 8}


def down_weights(scal, dc, wd, wbuf, sem, wanted):
    width = wbuf.shape[2]
    copies = {}
    for dy, dx in wanted:
        w = (dy & 1) * 4 + dx
        if w in copies:
            continue
        _, t = plane_target(scal, dc, dy, dx)
        cols = pl.ds(pl.multiple_of(t * width, 128), width)
        copies[w] = pltpu.make_async_copy(wd.at[:, cols], wbuf.at[w], sem.at[w])
        copies[w].start()
    return copies


def down_products(scal, dc, hidden, wbuf, copies, wanted):
    half = hidden.shape[1] // 2
    waited = set()
    for (dy, dx), (with_a, with_b) in wanted.items():
        w = (dy & 1) * 4 + dx
        if w not in waited:
            waited.add(w)
            copies[w].wait()
        pipe, _ = plane_target(scal, dc, dy, dx)
        if with_a and with_b:
            left = hidden[pipe]
        elif with_a:
            left = hidden[pipe, 0:half]
        else:
            left = hidden[pipe, half:]
        out = jnp.dot(left, wbuf[w], preferred_element_type=F32)
        a = out[0:half] if with_a else None
        b = (out[half:] if with_a else out) if with_b else None
        yield dy, dx, a, b


def down_far_kernel(scal, hidden, wd, first, later, wbuf, sem):
    wanted = {(dy, dx): (True, True) for dy in (2, 0, 1, 3) for dx in (2, 0, 1, 3)}
    copies = down_weights(scal, 1, wd, wbuf, sem, wanted)
    for dy, dx, a, b in down_products(scal, 1, hidden, wbuf, copies, wanted):
        if dy == 2:
            first[dx] = a.astype(BF)
        else:
            later[LATER[dy] + dx] = a.astype(BF)
        if dx == 2:
            first[4 + dy] = b.astype(BF)
        else:
            later[12 + LATER[dx] + dy] = b.astype(BF)


def down_first_kernel(scal, hidden, wd, got, a_lo, a_hi, b_lo, b_hi, wbuf, sem):
    wanted = {(2, 2): (True, True)}
    for j in (0, 1, 3):
        wanted[(2, j)] = (True, False)
        wanted[(j, 2)] = (False, True)
    copies = down_weights(scal, 0, wd, wbuf, sem, wanted)
    for dy, dx, a, b in down_products(scal, 0, hidden, wbuf, copies, wanted):
        if a is not None:
            a = (a + got[dx].astype(F32)).astype(BF)
            if dx < 2:
                a_lo[dx] = a
            else:
                a_hi[dx - 2] = a
        if b is not None:
            b = (b + got[4 + dy].astype(F32)).astype(BF)
            if dy < 2:
                b_lo[dy] = b
            else:
                b_hi[dy - 2] = b


def down_later_kernel(scal, hidden, wd, got, a1, a3, a0, b1, b3, b0, wbuf, sem):
    wanted = {}
    for dy in (1, 3, 0, 2):
        for dx in (1, 3, 0, 2):
            if dy != 2 or dx != 2:
                wanted[(dy, dx)] = (dy != 2, dx != 2)
    copies = down_weights(scal, 0, wd, wbuf, sem, wanted)
    a_out = {0: a0, 1: a1, 3: a3}
    b_out = {0: b0, 1: b1, 3: b3}
    for dy, dx, a, b in down_products(scal, 0, hidden, wbuf, copies, wanted):
        if a is not None:
            a_out[dy][dx] = (a + got[LATER[dy] + dx].astype(F32)).astype(BF)
        if b is not None:
            b_out[dx][dy] = (b + got[12 + LATER[dx] + dy].astype(F32)).astype(BF)


def down_call(kernel, counts, scal, hidden, wd, got=None):
    half = hidden.shape[1] // 2
    width = wd.shape[1] // N_TENSOR
    extra = [] if got is None else [got]
    return pl.pallas_call(
        kernel,
        out_shape=[jax.ShapeDtypeStruct((n, half, width), BF) for n in counts],
        in_specs=[IN_SMEM, IN_VMEM, ANY] + [IN_VMEM] * len(extra),
        out_specs=[IN_VMEM] * len(counts),
        scratch_shapes=[
            pltpu.VMEM((8, wd.shape[0], width), BF),
            pltpu.SemaphoreType.DMA((8,)),
        ],
        compiler_params=params(),
        name=kernel.__name__,
    )(scal, hidden, wd, *extra)


def expert_layer(scal, gains, arrived, wg, wu, wd):
    half = arrived.shape[0] // 2
    top, low = arrived[:half], arrived[half:]
    xa = jnp.stack([top] + [from_x(top, d) for d in (1, 2, 3)])
    yb = jnp.stack([low] + [from_plane(low, 0, d) for d in (1, 2, 3)])
    au, ad = from_plane(xa, 0, 1), from_plane(xa, 0, 3)
    bu, bd = from_x(yb, 1), from_x(yb, 3)
    ah0, ah1 = from_plane(au[:2], 0, 1), from_plane(ad[2:], 0, 3)
    bh0, bh1 = from_x(bu[:2], 1), from_x(bd[2:], 3)
    near = (xa, au, ad, ah0, ah1, yb, bu, bd, bh0, bh1)
    far = tuple(from_flip(v, 1) for v in near)
    hidden = gate_up(scal, gains, near, far, wg, wu)
    first, later = down_call(down_far_kernel, (8, 24), scal, hidden, wd)
    got_first, got_later = from_flip(first, 1), from_flip(later, 1)
    a_lo, a_hi, b_lo, b_hi = down_call(
        down_first_kernel, (2, 2, 2, 2), scal, hidden, wd, got_first
    )
    a1, a3, a0, b1, b3, b0 = down_call(
        down_later_kernel, (4,) * 6, scal, hidden, wd, got_later
    )

    def add(base, *parts):
        total = base.astype(F32)
        for part in parts:
            total = total + part.astype(F32)
        return total.astype(BF)

    ra_lo, ra_hi = from_plane(a_lo, 0, 3), from_plane(a_hi, 0, 1)
    rb_lo, rb_hi = from_x(b_lo, 3), from_x(b_hi, 1)
    a1 = jnp.concatenate([add(a1[:2], ra_lo), a1[2:]])
    a3 = jnp.concatenate([a3[:2], add(a3[2:], ra_hi)])
    b1 = jnp.concatenate([add(b1[:2], rb_lo), b1[2:]])
    b3 = jnp.concatenate([b3[:2], add(b3[2:], rb_hi)])
    a0 = add(a0, from_plane(a1, 0, 3), from_plane(a3, 0, 1))
    b0 = add(b0, from_x(b1, 3), from_x(b3, 1))
    top = add(a0[0], *(from_x(a0[d], 4 - d) for d in (1, 2, 3)))
    low = add(b0[0], *(from_plane(b0[d], 0, 4 - d) for d in (1, 2, 3)))
    return jnp.concatenate([top, low])


N_TOKEN_ARRAYS = 10


def load_tokens(scal, refs, wq, wk, wv, xt, wbuf, xsem, wsem):
    n0, u1, d1, u2, d2, u3, d3, n4, s0, s1, s2, s3, s4 = refs
    pieces = {0: n0, 1: u1, 7: d1, 2: u2, 6: d2, 3: u3, 5: d3, 4: n4}
    pieces.update({8: s0, 9: s1.at[0], 15: s1.at[1], 10: s2.at[0], 14: s2.at[1]})
    pieces.update({11: s3.at[0], 13: s3.at[1], 12: s4})
    copies = []
    for i, ref in sorted(pieces.items()):
        copies.append(pltpu.make_async_copy(ref, xt.at[i], xsem.at[i]))
    qw = wq.shape[1]
    head = pl.ds(pl.multiple_of(scal[4] * HD, HD), HD)
    copies.append(pltpu.make_async_copy(wq, wbuf.at[:, pl.ds(0, qw)], wsem.at[0]))
    copies.append(
        pltpu.make_async_copy(wk.at[:, head], wbuf.at[:, pl.ds(qw, HD)], wsem.at[1])
    )
    copies.append(
        pltpu.make_async_copy(wv.at[:, head], wbuf.at[:, pl.ds(qw + HD, HD)], wsem.at[2])
    )
    for copy in copies:
        copy.start()
    for copy in copies:
        copy.wait()


def tensor_target(scal, dc, dl, dx):
    t = scal[0]
    tx = lax.bitwise_and(lax.shift_right_logical(t, 2) + dx, 3)
    return tx * 4 + lax.bitwise_xor(lax.bitwise_and(t, 3), dl * 2 + dc)


def projected(scal, dc, gain, xt, wbuf, sq_out):
    ones = jnp.ones((8, xt.shape[2]), F32)
    for dl in (1, 0):
        for dx in (1, 2, 3, 0):
            t = tensor_target(scal, dc, dl, dx)
            dp = lax.bitwise_xor(lax.shift_right_logical(t, 3), scal[2])
            dz = lax.bitwise_and(lax.bitwise_and(t, 7) - scal[3] + 8, 7)
            rows = xt[dp * 8 + dz].astype(F32)
            squares = lax.dot_general(
                ones,
                rows * rows,
                (((1,), (1,)), ((), ())),
                precision=lax.Precision.HIGHEST,
                preferred_element_type=F32,
            )
            at = dl * 4 + dx
            sq_out[at : at + 1, :] = squares[0:1]
            left = (rows * gain[...]).astype(BF)
            yield dl, dx, jnp.dot(left, wbuf[...], preferred_element_type=F32)


def proj_far_kernel(scal, gain, *refs):
    tokens, (wq, wk, wv, out, sq_out, xt, wbuf, xsem, wsem) = refs[:13], refs[13:]
    load_tokens(scal, tokens, wq, wk, wv, xt, wbuf, xsem, wsem)
    for dl, dx, product in projected(scal, 1, gain, xt, wbuf, sq_out):
        out[dl * 4 + dx] = product.astype(BF)


def proj_near_kernel(scal, gain, got, *refs):
    tokens = refs[:13]
    wq, wk, wv, ay1, ay0, bx1, bx2, bx3, bx0, sq_out, xt, wbuf, xsem, wsem = refs[13:]
    load_tokens(scal, tokens, wq, wk, wv, xt, wbuf, xsem, wsem)
    half = xt.shape[1] // 2
    ay = (ay0, ay1)
    bx = (bx0, bx1, bx2, bx3)
    for dl, dx, product in projected(scal, 0, gain, xt, wbuf, sq_out):
        total = (product + got[dl * 4 + dx].astype(F32)).astype(BF)
        ay[dl][dx] = total[:half]
        bx[dx][dl] = total[half:]


def proj_call(kernel, shapes, scal, gain, tokens, wq, wk, wv, got=None):
    rows, width = tokens[0].shape
    columns = wq.shape[1] + 2 * HD
    extra = [] if got is None else [got]
    return pl.pallas_call(
        kernel,
        out_shape=[jax.ShapeDtypeStruct(s + (columns,), BF) for s in shapes]
        + [jax.ShapeDtypeStruct((8, rows), F32)],
        in_specs=[IN_SMEM, IN_VMEM] + [IN_VMEM] * len(extra) + [ANY] * 16,
        out_specs=[IN_VMEM] * (len(shapes) + 1),
        scratch_shapes=[
            pltpu.VMEM((16, rows, width), BF),
            pltpu.VMEM((width, columns), BF),
            pltpu.SemaphoreType.DMA((16,)),
            pltpu.SemaphoreType.DMA((3,)),
        ],
        compiler_params=params(),
        name=kernel.__name__,
    )(scal, gain, *extra, *tokens, wq, wk, wv)


def attend_kernel(scal, q, kv0, kv1, out):
    rows = q.shape[0]
    heads = q.shape[1] // HD
    own = scal[0]
    keys, values, places = [], [], []
    for dc, kv in enumerate((kv0, kv1)):
        for dl in range(2):
            for dx in range(4):
                block = kv[dl * 4 + dx]
                keys.append(block[:, :HD])
                values.append(block[:, HD:])
                base = tensor_target(scal, dc, dl, dx) * rows
                places.append(lax.broadcasted_iota(jnp.int32, (rows, rows), 1) + base)
    keys = jnp.concatenate(keys, axis=0)
    values = jnp.concatenate(values, axis=0)
    places = jnp.concatenate(places, axis=1)
    mine = lax.broadcasted_iota(jnp.int32, places.shape, 0) + own * rows
    allowed = places <= mine
    for h in range(heads):
        scores = lax.dot_general(
            q[:, h * HD : (h + 1) * HD],
            keys,
            (((1,), (1,)), ((), ())),
            preferred_element_type=F32,
        ) * (1.0 / math.sqrt(HD))
        scores = jnp.where(allowed, scores, -1e30)
        best = jnp.max(scores, axis=1, keepdims=True)
        weights = jnp.where(allowed, jnp.exp(scores - best), 0.0)
        total = jnp.sum(weights, axis=1, keepdims=True)
        mixed = jnp.dot(weights.astype(BF), values, preferred_element_type=F32)
        out[:, h * HD : (h + 1) * HD] = (mixed / total).astype(BF)


def attend(scal, q, kv0, kv1):
    return pl.pallas_call(
        attend_kernel,
        out_shape=jax.ShapeDtypeStruct(q.shape, BF),
        in_specs=[IN_SMEM] + [IN_VMEM] * 3,
        out_specs=IN_VMEM,
        compiler_params=params(),
        name="attend",
    )(scal, q, kv0, kv1)


def gather_tokens(own):
    half = own.shape[0] // 2
    s0 = from_pipe(own)
    u1, d1 = from_z(own, 1), from_z(own, 7)
    s1 = from_pipe(jnp.stack([u1, d1]))
    u2, d2 = from_z(u1, 1), from_z(d1, 7)
    s2 = from_pipe(jnp.stack([u2, d2]))
    u3, d3 = from_z(u2, 1), from_z(d2, 7)
    s3 = from_pipe(jnp.stack([u3, d3]))
    n4 = jnp.concatenate([from_z(u3[:half], 1), from_z(d3[half:], 7)])
    s4 = from_pipe(n4)
    return (own, u1, d1, u2, d2, u3, d3, n4, s0, s1, s2, s3, s4)


def on_device(
    stream,
    norm_gain,
    attn_gain,
    router,
    expert_ids,
    expert_slots,
    w_gate,
    w_up,
    w_down,
    w_query,
    w_key,
    w_value,
):
    token_rows, width = stream.shape
    features = width * N_TENSOR
    experts = router.shape[1]
    query_width = w_query.shape[1]
    heads_here = query_width // HD
    t = lax.axis_index("tensor")
    pipe = lax.axis_index("pipe")
    z = lax.axis_index("expert")
    kv_head = (pipe * 8 + z) * heads_here // (QH // KVH)
    yy = pipe * 2 + (t // 2) % 2
    scal = jnp.stack([t, yy, pipe, z, kv_head]).astype(jnp.int32)

    slot_total = experts * CAP
    target = jnp.where(expert_slots >= 0, expert_ids * CAP + expert_slots, slot_total)
    slots = jnp.arange(slot_total, dtype=jnp.int32)
    chosen = (slots[:, None] == target[:, 0][None]) | (slots[:, None] == target[:, 1][None])
    outgoing = jnp.dot(chosen.astype(BF), stream, preferred_element_type=F32).astype(BF)
    arrived = lax.all_to_all(outgoing, "expert", split_axis=0, concat_axis=0, tiled=True)

    stream_f = stream.astype(F32)
    logit_part = lax.dot_general(
        router, stream_f * norm_gain, (((0,), (1,)), ((), ())), precision=lax.Precision.HIGHEST
    )
    square_part = jnp.sum(stream_f * stream_f, axis=1)
    sums = jnp.concatenate([logit_part, square_part[None]])
    gains = norm_gain.reshape(1, width // 128, 128)
    for bit in (1, 2, 4, 8):
        sent = jnp.concatenate([sums, gains.reshape(-1, 128)])
        got = from_flip(sent, bit)
        sums = sums + got[: experts + 1]
        gains = jnp.concatenate([gains, got[experts + 1 :].reshape(gains.shape)])
    gains = gains.reshape(N_TENSOR, 1, width)

    expert_out = expert_layer(scal, gains, arrived, w_gate[0], w_up[0], w_down[0])
    returned = lax.all_to_all(expert_out, "expert", split_axis=0, concat_axis=0, tiled=True)

    inverse = lax.rsqrt(sums[experts] / features + NORM_EPS)
    logits = inverse[None, :] * sums[:experts]
    numbers = jnp.arange(experts, dtype=jnp.int32)[:, None]
    first_logit = jnp.sum(jnp.where(numbers == expert_ids[:, 0][None], logits, 0.0), axis=0)
    second_logit = jnp.sum(jnp.where(numbers == expert_ids[:, 1][None], logits, 0.0), axis=0)
    first_share = jax.nn.sigmoid(first_logit - second_logit)
    second_share = 1.0 - first_share

    wanted = jnp.concatenate([target[:, 0], target[:, 1]])
    picks = (wanted[:, None] == slots[None]).astype(BF)
    picked = jnp.dot(picks, returned, preferred_element_type=F32)
    moe_sum = (
        first_share[:, None] * picked[:token_rows] + second_share[:, None] * picked[token_rows:]
    )
    new_stream = (stream_f + moe_sum).astype(BF)

    tokens = gather_tokens(new_stream)
    gain = attn_gain.reshape(1, width)
    far, sq_far = proj_call(
        proj_far_kernel, [(8, token_rows)], scal, gain, tokens, w_query, w_key, w_value
    )
    got = from_flip(far, 1)
    got_sq = from_flip(sq_far, 1)
    hr = token_rows // 2
    ay1, ay0, bx1, bx2, bx3, bx0, sq = proj_call(
        proj_near_kernel,
        [(4, hr), (4, hr), (2, hr), (2, hr), (2, hr), (2, hr)],
        scal,
        gain,
        tokens,
        w_query,
        w_key,
        w_value,
        got,
    )
    sq = sq + got_sq
    sq = sq[:4] + from_flip(sq[4:], 2)
    sq = sq[0] + sum(from_x(sq[d : d + 1], 4 - d)[0] for d in (1, 2, 3))

    a = (ay0.astype(F32) + from_flip(ay1, 2).astype(F32)).astype(BF)
    b = bx0.astype(F32)
    for d, part in ((1, bx1), (2, bx2), (3, bx3)):
        b = b + from_x(part, 4 - d).astype(F32)
    b = b.astype(BF)
    a_sum = a[0].astype(F32)
    for d in (1, 2, 3):
        a_sum = a_sum + from_x(a[d], 4 - d).astype(F32)
    b_sum = b[0].astype(F32) + from_flip(b[1], 2).astype(F32)
    own_proj = jnp.concatenate([a_sum, b_sum])
    inverse_two = lax.rsqrt(sq / features + NORM_EPS)[:, None]
    own_proj = jnp.where(inverse_two > 0.0, own_proj * inverse_two, 0.0).astype(BF)
    queries = own_proj[:, :query_width]
    kv = own_proj[:, query_width:]
    kv = jnp.stack([kv] + [from_x(kv, d) for d in (1, 2, 3)])
    kv = jnp.concatenate([kv, from_flip(kv, 2)])
    attended = attend(scal, queries, kv, from_flip(kv, 1))
    return (new_stream, attended)


def solution(mesh):
    in_specs = (
        P(("pipe", "expert"), "tensor"),
        P("tensor"),
        P("tensor"),
        P("tensor", None),
        P(("pipe", "expert"), None),
        P(("pipe", "expert"), None),
        P("expert", None, ("pipe", "tensor")),
        P("expert", None, ("pipe", "tensor")),
        P("expert", ("pipe", "tensor"), None),
        P("tensor", ("pipe", "expert")),
        P("tensor", None),
        P("tensor", None),
    )
    out_specs = (P(("pipe", "expert"), "tensor"), P("tensor", ("pipe", "expert")))
    return jax.shard_map(
        on_device, mesh=mesh, in_specs=in_specs, out_specs=out_specs, check_vma=False
    )
```

```python
import math

import jax
import jax.numpy as jnp
from jax import lax
from jax.experimental import pallas as pl
from jax.experimental.pallas import tpu as pltpu
from jax.sharding import PartitionSpec as P

HD = 128
QH = 48
KVH = 8
CAP = 40
NORM_EPS = 1e-05
N_TENSOR = 16
BF = jnp.bfloat16
F32 = jnp.float32


def from_plane(value, dx, dy):
    pairs = []
    for x in range(4):
        for yy in range(4):
            for core in range(2):
                source = (yy // 2) * 16 + x * 4 + (yy % 2) * 2 + core
                tx, ty = (x - dx) % 4, (yy - dy) % 4
                pairs.append((source, (ty // 2) * 16 + tx * 4 + (ty % 2) * 2 + core))
    return lax.ppermute(value, ("pipe", "tensor"), pairs)


def from_x(value, dx):
    pairs = [(i, (i - 4 * dx) % 16) for i in range(16)]
    return lax.ppermute(value, "tensor", pairs)


def from_flip(value, bit):
    return lax.ppermute(value, "tensor", [(i, i ^ bit) for i in range(16)])


def from_z(value, dz):
    return lax.ppermute(value, "expert", [(i, (i - dz) % 8) for i in range(8)])


def from_pipe(value):
    return lax.ppermute(value, "pipe", [(0, 1), (1, 0)])


def place(scal):
    t = scal[0]
    yy = scal[1]
    return lax.shift_right_logical(t, 2), yy, lax.bitwise_and(t, 1)


def plane_target(scal, dc, dy, dx):
    x, yy, core = place(scal)
    tx = lax.bitwise_and(x + dx, 3)
    ty = lax.bitwise_and(yy + dy, 3)
    pipe = lax.shift_right_logical(ty, 1)
    tensor = tx * 4 + lax.bitwise_and(ty, 1) * 2 + lax.bitwise_xor(core, dc)
    return pipe, tensor


def sigmoid(v):
    return 1.0 / (1.0 + jnp.exp(-v))


def split3(value):
    high = lax.reduce_precision(value, 8, 7)
    rest = value - high
    middle = lax.reduce_precision(rest, 8, 7)
    return high.astype(BF), middle.astype(BF), (rest - middle).astype(BF)


def gate_up_kernel(scal, *refs):
    near, far = refs[0:8], refs[8:16]
    wg, wu, hidden, acc, ssq = refs[16:]
    width = near[0].shape[-1]
    half = near[4].shape[1]
    columns = wg.shape[1]
    acc[...] = jnp.zeros_like(acc)
    ssq[...] = jnp.zeros_like(ssq)
    for parity in range(2):
        for dx in range(4):
            scaled, weights = [], []
            squares = 0.0
            for dc, table in enumerate((near, far)):
                pipe, t = plane_target(scal, dc, parity, dx)
                rows = []
                for dy in (parity, parity + 2):
                    rows += [table[dy][dx, 0:half], table[4 + dx][dy]]
                rows = jnp.concatenate(rows, axis=0).astype(F32)
                parts = table[parity][dx, half : half + 16].astype(F32)
                gain = parts[0:1] + parts[1:2] + parts[2:3]
                scaled.append((rows * gain).astype(BF))
                rows = rows * rows
                for j in range(width // 128):
                    squares = squares + rows[:, j * 128 : (j + 1) * 128]
                weights.append(pl.ds(pl.multiple_of(t * width, 128), width))
            left = jnp.concatenate(scaled, axis=1)
            gate_w = jnp.concatenate([wg[rows, :] for rows in weights], axis=0)
            up_w = jnp.concatenate([wu[rows, :] for rows in weights], axis=0)
            gate = jnp.dot(left, gate_w, preferred_element_type=F32)
            up = jnp.dot(left, up_w, preferred_element_type=F32)
            for part, at in enumerate((pipe, 1 - pipe)):
                here = slice(part * 2 * half, (part + 1) * 2 * half)
                acc[at, :, 0:columns] += gate[here]
                acc[at, :, columns:] += up[here]
                ssq[at] += squares[here]
    for pipe in range(2):
        total = jnp.sum(ssq[pipe], axis=1, keepdims=True)
        inverse = lax.rsqrt(total / (width * N_TENSOR) + NORM_EPS)
        keep = inverse > 0.0
        gate = jnp.where(keep, acc[pipe, :, 0:columns] * inverse, 0.0)
        up = jnp.where(keep, acc[pipe, :, columns:] * inverse, 0.0)
        hidden[pipe] = (gate * sigmoid(gate) * up).astype(BF)


IN_VMEM = pl.BlockSpec(memory_space=pltpu.VMEM)
IN_SMEM = pl.BlockSpec(memory_space=pltpu.SMEM)


def params(mib):
    return pltpu.CompilerParams(vmem_limit_bytes=mib * 1024 * 1024)


def gate_up(scal, near, far, wg, wu):
    rows = near[4].shape[1] * 2
    columns = wg.shape[1]
    return pl.pallas_call(
        gate_up_kernel,
        out_shape=jax.ShapeDtypeStruct((2, rows, columns), BF),
        in_specs=[IN_SMEM] + [IN_VMEM] * 18,
        out_specs=IN_VMEM,
        scratch_shapes=[
            pltpu.VMEM((2, rows, 2 * columns), F32),
            pltpu.VMEM((2, rows, 128), F32),
        ],
        compiler_params=params(28),
        name="gate_up",
    )(scal, *near, *far, wg, wu)


LATER = {0: 0, 1: 4, 3: 8}
FIRST_PIECES = {(2, 2): (True, True)}
LATER_PIECES = {}
for _j in (0, 1, 3):
    FIRST_PIECES[(2, _j)] = (True, False)
    FIRST_PIECES[(_j, 2)] = (False, True)
for _dy in (1, 3, 0, 2):
    for _dx in (1, 3, 0, 2):
        if _dy != 2 or _dx != 2:
            LATER_PIECES[(_dy, _dx)] = (_dy != 2, _dx != 2)


def down_products(scal, dc, hidden, wd, wanted):
    half = hidden.shape[1] // 2
    width = wd.shape[1] // N_TENSOR
    for (dy, dx), (with_a, with_b) in wanted.items():
        pipe, t = plane_target(scal, dc, dy, dx)
        if with_a and with_b:
            left = hidden[pipe]
        elif with_a:
            left = hidden[pipe, 0:half]
        else:
            left = hidden[pipe, half:]
        cols = pl.ds(pl.multiple_of(t * width, 128), width)
        out = jnp.dot(left, wd[:, cols], preferred_element_type=F32)
        a = out[0:half] if with_a else None
        b = (out[half:] if with_a else out) if with_b else None
        yield dy, dx, a, b


def far_first_kernel(scal, hidden, wd, out):
    for dy, dx, a, b in down_products(scal, 1, hidden, wd, FIRST_PIECES):
        if a is not None:
            out[dx] = a.astype(BF)
        if b is not None:
            out[4 + dy] = b.astype(BF)


def far_later_kernel(scal, hidden, wd, out):
    for dy, dx, a, b in down_products(scal, 1, hidden, wd, LATER_PIECES):
        if a is not None:
            out[LATER[dy] + dx] = a.astype(BF)
        if b is not None:
            out[12 + LATER[dx] + dy] = b.astype(BF)


def near_first_kernel(scal, hidden, wd, got, a2, b2):
    for dy, dx, a, b in down_products(scal, 0, hidden, wd, FIRST_PIECES):
        if a is not None:
            a2[dx] = (a + got[dx].astype(F32)).astype(BF)
        if b is not None:
            b2[dy] = (b + got[4 + dy].astype(F32)).astype(BF)


def near_later_kernel(scal, hidden, wd, got, a1, a3, a0, b1, b3, b0):
    a_out = {0: a0, 1: a1, 3: a3}
    b_out = {0: b0, 1: b1, 3: b3}
    for dy, dx, a, b in down_products(scal, 0, hidden, wd, LATER_PIECES):
        if a is not None:
            a_out[dy][dx] = (a + got[LATER[dy] + dx].astype(F32)).astype(BF)
        if b is not None:
            b_out[dx][dy] = (b + got[12 + LATER[dx] + dy].astype(F32)).astype(BF)


def down_call(kernel, counts, scal, hidden, wd, *got):
    half = hidden.shape[1] // 2
    width = wd.shape[1] // N_TENSOR
    return pl.pallas_call(
        kernel,
        out_shape=[jax.ShapeDtypeStruct((n, half, width), BF) for n in counts],
        in_specs=[IN_SMEM] + [IN_VMEM] * (2 + len(got)),
        out_specs=[IN_VMEM] * len(counts),
        compiler_params=params(20),
        name=kernel.__name__,
    )(scal, hidden, wd, *got)


def add(base, *parts):
    total = base.astype(F32)
    for part in parts:
        total = total + part.astype(F32)
    return total.astype(BF)


def expert_layer(scal, gain_rows, arrived, wg, wu, wd):
    half = arrived.shape[0] // 2
    top, low = jnp.concatenate([arrived[:half], gain_rows]), arrived[half:]
    xa = jnp.stack([top] + [from_x(top, d) for d in (1, 2, 3)])
    yb = jnp.stack([low] + [from_plane(low, 0, d) for d in (1, 2, 3)])
    near = [xa] + [from_plane(xa, 0, d) for d in (1, 2, 3)]
    near += [yb] + [from_x(yb, d) for d in (1, 2, 3)]
    far = [from_flip(v, 1) for v in near]
    hidden = gate_up(scal, near, far, wg, wu)
    (first,) = down_call(far_first_kernel, (8,), scal, hidden, wd)
    got_first = from_flip(first, 1)
    (later,) = down_call(far_later_kernel, (24,), scal, hidden, wd)
    got_later = from_flip(later, 1)
    a2, b2 = down_call(near_first_kernel, (4, 4), scal, hidden, wd, got_first)
    a1, a3, a0, b1, b3, b0 = down_call(near_later_kernel, (4,) * 6, scal, hidden, wd, got_later)
    a = add(a0, from_plane(a1, 0, 3), from_plane(a2, 0, 2), from_plane(a3, 0, 1))
    b = add(b0, from_x(b1, 3), from_x(b2, 2), from_x(b3, 1))
    top = add(a[0], *(from_x(a[d], 4 - d) for d in (1, 2, 3)))
    low = add(b[0], *(from_plane(b[d], 0, 4 - d) for d in (1, 2, 3)))
    return jnp.concatenate([top, low])


CORE_GROUPS = [list(range(0, 16, 2)), list(range(1, 16, 2))]


def exchange(value):
    return lax.all_to_all(
        value, "tensor", split_axis=0, concat_axis=0, axis_index_groups=CORE_GROUPS
    )


def product_blocks(scal, core, xt, wbuf):
    rows = xt.shape[1]
    for group in range(2):
        slots = []
        for j in range(group * 4, group * 4 + 4):
            t = j * 2 + core
            dp = lax.bitwise_xor(lax.shift_right_logical(t, 3), scal[2])
            dz = lax.bitwise_and(lax.bitwise_and(t, 7) - scal[3] + 8, 7)
            slots.append(dp * 8 + dz)
        left = jnp.concatenate([xt[slot] for slot in slots], axis=0)
        product = jnp.dot(left, wbuf[...], preferred_element_type=F32)
        for k, slot in enumerate(slots):
            yield group * 4 + k, slot, product[k * rows : (k + 1) * rows]


def store_block(out, j, product, squares):
    rows = product.shape[0]
    out[j, 0:rows] = product.astype(BF)
    high = squares.astype(BF)
    rest = squares - high.astype(F32)
    middle = rest.astype(BF)
    low = (rest - middle.astype(F32)).astype(BF)
    empty = jnp.zeros((16, product.shape[1] - 3 * rows), BF)
    wide = [jnp.broadcast_to(v.astype(F32), (16, rows)).astype(BF) for v in (high, middle, low)]
    out[j, rows : rows + 16] = jnp.concatenate(wide + [empty], axis=1)


def proj_far_kernel(scal, gain, *refs):
    n0, u1, d1, u2, d2, u3, d3, h4, l4, s0, s1, s2 = refs[:12]
    wq, wk, wv, out, xt, sq, wbuf = refs[12:]
    half = h4.shape[0]
    n4 = jnp.concatenate([h4[...], l4[...]], axis=0)
    pieces = {0: n0, 1: u1, 7: d1, 2: u2, 6: d2, 3: u3, 5: d3, 8: s0}
    pieces = {i: ref[...] for i, ref in pieces.items()}
    pieces.update({4: n4, 9: s1[0], 15: s1[1], 10: s1[2], 14: s1[3]})
    pieces.update({11: s2[0], 13: s2[1], 12: s2[2]})
    ones = jnp.ones((8, n0.shape[1]), F32)
    for i, value in pieces.items():
        rows = value.astype(F32)
        xt[i] = (rows * gain[...]).astype(BF)
        sq[i] = lax.dot_general(
            ones,
            rows * rows,
            (((1,), (1,)), ((), ())),
            precision=lax.Precision.HIGHEST,
            preferred_element_type=F32,
        )
    qw = wq.shape[1]
    head = pl.ds(pl.multiple_of(scal[4] * HD, HD), HD)
    wbuf[:, 0:qw] = wq[...]
    wbuf[:, qw : qw + HD] = wk[:, head]
    wbuf[:, qw + HD :] = wv[:, head]
    core = 1 - lax.bitwise_and(scal[0], 1)
    for j, slot, product in product_blocks(scal, core, xt, wbuf):
        store_block(out, j, product, sq[slot][0:1])


def proj_near_kernel(scal, got, xt, sq, wbuf, out):
    rows = xt.shape[1]
    core = lax.bitwise_and(scal[0], 1)
    for j, slot, product in product_blocks(scal, core, xt, wbuf):
        parts = got[j, rows : rows + 16].astype(F32)
        squares = sq[slot][0:1]
        for k in (2, 1, 0):
            squares = squares + parts[0:1, k * rows : (k + 1) * rows]
        store_block(out, j, product + got[j, 0:rows].astype(F32), squares)


def projections(scal, gain, tokens, wq, wk, wv):
    rows, width = tokens[0].shape
    columns = wq.shape[1] + 2 * HD
    sums = jax.ShapeDtypeStruct((8, rows + 16, columns), BF)
    far, xt, sq, wbuf = pl.pallas_call(
        proj_far_kernel,
        out_shape=[
            sums,
            jax.ShapeDtypeStruct((16, rows, width), BF),
            jax.ShapeDtypeStruct((16, 8, rows), F32),
            jax.ShapeDtypeStruct((width, columns), BF),
        ],
        in_specs=[IN_SMEM] + [IN_VMEM] * 16,
        out_specs=[IN_VMEM] * 4,
        compiler_params=params(20),
        name="proj_far",
    )(scal, gain, *tokens, wq, wk, wv)
    got = from_flip(far, 1)
    near = pl.pallas_call(
        proj_near_kernel,
        out_shape=sums,
        in_specs=[IN_SMEM] + [IN_VMEM] * 4,
        out_specs=IN_VMEM,
        compiler_params=params(20),
        name="proj_near",
    )(scal, got, xt, sq, wbuf)
    total = jnp.sum(exchange(near).astype(F32), axis=0)
    parts = total[rows, : 3 * rows].reshape(3, rows)
    return total[:rows], parts[0] + (parts[1] + parts[2])


def attend_kernel(scal, q, kv0, kv1, out):
    rows = q.shape[0]
    heads = q.shape[1] // HD
    own = scal[0]
    core = lax.bitwise_and(own, 1)
    keys, values, places = [], [], []
    for dc, kv in enumerate((kv0, kv1)):
        for j in range(8):
            block = kv[j]
            keys.append(block[:, :HD])
            values.append(block[:, HD:])
            base = (2 * j + lax.bitwise_xor(core, dc)) * rows
            places.append(lax.broadcasted_iota(jnp.int32, (rows, rows), 1) + base)
    keys = jnp.concatenate(keys, axis=0)
    values = jnp.concatenate(values, axis=0)
    places = jnp.concatenate(places, axis=1)
    mine = lax.broadcasted_iota(jnp.int32, places.shape, 0) + own * rows
    allowed = places <= mine
    for h in range(heads):
        scores = lax.dot_general(
            q[:, h * HD : (h + 1) * HD],
            keys,
            (((1,), (1,)), ((), ())),
            preferred_element_type=F32,
        ) * (1.0 / math.sqrt(HD))
        scores = jnp.where(allowed, scores, -1e30)
        best = jnp.max(scores, axis=1, keepdims=True)
        weights = jnp.where(allowed, jnp.exp(scores - best), 0.0)
        total = jnp.sum(weights, axis=1, keepdims=True)
        mixed = jnp.dot(weights.astype(BF), values, preferred_element_type=F32)
        out[:, h * HD : (h + 1) * HD] = (mixed / total).astype(BF)


def attend(scal, q, kv0, kv1):
    return pl.pallas_call(
        attend_kernel,
        out_shape=jax.ShapeDtypeStruct(q.shape, BF),
        in_specs=[IN_SMEM] + [IN_VMEM] * 3,
        out_specs=IN_VMEM,
        compiler_params=params(24),
        name="attend",
    )(scal, q, kv0, kv1)


def gather_tokens(own):
    half = own.shape[0] // 2
    s0 = from_pipe(own)
    u1, d1, u2, d2 = (from_z(own, d) for d in (1, 7, 2, 6))
    s1 = from_pipe(jnp.stack([u1, d1, u2, d2]))
    u3, d3 = from_z(u2, 1), from_z(d2, 7)
    h4, l4 = from_z(u2[:half], 2), from_z(d2[half:], 6)
    s2 = from_pipe(jnp.stack([u3, d3, jnp.concatenate([h4, l4])]))
    return (own, u1, d1, u2, d2, u3, d3, h4, l4, s0, s1, s2)


def on_device(
    stream,
    norm_gain,
    attn_gain,
    router,
    expert_ids,
    expert_slots,
    w_gate,
    w_up,
    w_down,
    w_query,
    w_key,
    w_value,
):
    token_rows, width = stream.shape
    features = width * N_TENSOR
    experts = router.shape[1]
    query_width = w_query.shape[1]
    heads_here = query_width // HD
    t = lax.axis_index("tensor")
    pipe = lax.axis_index("pipe")
    z = lax.axis_index("expert")
    kv_head = (pipe * 8 + z) * heads_here // (QH // KVH)
    yy = pipe * 2 + (t // 2) % 2
    scal = jnp.stack([t, yy, pipe, z, kv_head]).astype(jnp.int32)

    slot_total = experts * CAP
    target = jnp.where(expert_slots >= 0, expert_ids * CAP + expert_slots, slot_total)
    slots = jnp.arange(slot_total, dtype=jnp.int32)
    chosen = (slots[:, None] == target[:, 0][None]) | (slots[:, None] == target[:, 1][None])
    outgoing = jnp.dot(chosen.astype(BF), stream, preferred_element_type=F32).astype(BF)
    arrived = lax.all_to_all(outgoing, "expert", split_axis=0, concat_axis=0, tiled=True)

    stream_f = stream.astype(F32)
    logit_part = lax.dot_general(
        router, stream_f * norm_gain, (((0,), (1,)), ((), ())), precision=lax.Precision.HIGHEST
    )
    numbers = jnp.arange(experts, dtype=jnp.int32)[:, None]
    first_one = (numbers == expert_ids[:, 0][None]).astype(F32)
    second_one = (numbers == expert_ids[:, 1][None]).astype(F32)
    apart_part = jnp.sum(jnp.where(first_one > 0.0, logit_part, 0.0), axis=0) - jnp.sum(
        jnp.where(second_one > 0.0, logit_part, 0.0), axis=0
    )
    sums = jnp.stack([jnp.sum(stream_f * stream_f, axis=1), apart_part])
    for bit in (1, 2, 4, 8):
        sums = sums + from_flip(sums, bit)

    gain_rows = jnp.stack(split3(norm_gain))
    gain_rows = jnp.concatenate([gain_rows, jnp.zeros((13, width), BF)])
    expert_out = expert_layer(scal, gain_rows, arrived, w_gate[0], w_up[0], w_down[0])
    returned = lax.all_to_all(expert_out, "expert", split_axis=0, concat_axis=0, tiled=True)

    inverse = lax.rsqrt(sums[0] / features + NORM_EPS)
    first_share = jax.nn.sigmoid(inverse * sums[1])
    second_share = 1.0 - first_share

    wanted = jnp.concatenate([target[:, 0], target[:, 1]])
    picks = (wanted[:, None] == slots[None]).astype(BF)
    picked = jnp.dot(picks, returned, preferred_element_type=F32)
    moe_sum = (
        first_share[:, None] * picked[:token_rows] + second_share[:, None] * picked[token_rows:]
    )
    new_stream = (stream_f + moe_sum).astype(BF)

    tokens = gather_tokens(new_stream)
    own_proj, squares_two = projections(
        scal, attn_gain.reshape(1, width), tokens, w_query, w_key, w_value
    )
    inverse_two = lax.rsqrt(squares_two / features + NORM_EPS)[:, None]
    own_proj = jnp.where(inverse_two > 0.0, own_proj * inverse_two, 0.0).astype(BF)
    queries = own_proj[:, :query_width]
    kv = own_proj[:, query_width:]
    kv = exchange(jnp.broadcast_to(kv[None], (8,) + kv.shape))
    attended = attend(scal, queries, kv, from_flip(kv, 1))
    return (new_stream, attended)


def solution(mesh):
    in_specs = (
        P(("pipe", "expert"), "tensor"),
        P("tensor"),
        P("tensor"),
        P("tensor", None),
        P(("pipe", "expert"), None),
        P(("pipe", "expert"), None),
        P("expert", None, ("pipe", "tensor")),
        P("expert", None, ("pipe", "tensor")),
        P("expert", ("pipe", "tensor"), None),
        P("tensor", ("pipe", "expert")),
        P("tensor", None),
        P("tensor", None),
    )
    out_specs = (P(("pipe", "expert"), "tensor"), P("tensor", ("pipe", "expert")))
    return jax.shard_map(
        on_device, mesh=mesh, in_specs=in_specs, out_specs=out_specs, check_vma=False
    )
```

```python
import functools
import math

import jax
import jax.numpy as jnp
from jax import lax
from jax.experimental import pallas as pl
from jax.experimental.pallas import tpu as pltpu
from jax.sharding import PartitionSpec as P

HD = 128
QH = 48
KVH = 8
CAP = 40
NORM_EPS = 1e-05
N_TENSOR = 16
BF = jnp.bfloat16
F32 = jnp.float32


def from_plane(value, dx, dy):
    pairs = []
    for x in range(4):
        for yy in range(4):
            for core in range(2):
                source = (yy // 2) * 16 + x * 4 + (yy % 2) * 2 + core
                tx, ty = (x - dx) % 4, (yy - dy) % 4
                pairs.append((source, (ty // 2) * 16 + tx * 4 + (ty % 2) * 2 + core))
    return lax.ppermute(value, ("pipe", "tensor"), pairs)


def from_x(value, dx):
    pairs = [(i, (i - 4 * dx) % 16) for i in range(16)]
    return lax.ppermute(value, "tensor", pairs)


def from_flip(value, bit):
    return lax.ppermute(value, "tensor", [(i, i ^ bit) for i in range(16)])


def from_z(value, dz):
    return lax.ppermute(value, "expert", [(i, (i - dz) % 8) for i in range(8)])


def from_pipe(value):
    return lax.ppermute(value, "pipe", [(0, 1), (1, 0)])


def place(scal):
    t = scal[0]
    yy = scal[1]
    return lax.shift_right_logical(t, 2), yy, lax.bitwise_and(t, 1)


def plane_target(scal, dc, dy, dx):
    x, yy, core = place(scal)
    tx = lax.bitwise_and(x + dx, 3)
    ty = lax.bitwise_and(yy + dy, 3)
    pipe = lax.shift_right_logical(ty, 1)
    tensor = tx * 4 + lax.bitwise_and(ty, 1) * 2 + lax.bitwise_xor(core, dc)
    return pipe, tensor


def sigmoid(v):
    return 1.0 / (1.0 + jnp.exp(-v))


def split3(value):
    high = lax.reduce_precision(value, 8, 7)
    rest = value - high
    middle = lax.reduce_precision(rest, 8, 7)
    return high.astype(BF), middle.astype(BF), (rest - middle).astype(BF)


def gate_up_kernel(scal, *refs):
    near, far = refs[0:8], refs[8:16]
    wg, wu, hidden, sums, acc, ssq, tok = refs[16:]
    width = near[0].shape[-1]
    half = near[4].shape[1]
    columns = wg.shape[1]
    acc[...] = jnp.zeros_like(acc)
    ssq[...] = jnp.zeros_like(ssq)
    tok[...] = jnp.zeros_like(tok)
    for parity in range(2):
        for dx in range(4):
            scaled, weights = [], []
            squares = 0.0
            for dc, table in enumerate((near, far)):
                pipe, t = plane_target(scal, dc, parity, dx)
                rows = []
                for dy in (parity, parity + 2):
                    rows += [table[dy][dx, 0:half], table[4 + dx][dy]]
                rows = jnp.concatenate(rows, axis=0).astype(F32)
                for k, dy in enumerate((parity, parity + 2)):
                    parts = table[dy][dx, half : half + 16].astype(F32)
                    if k == 0:
                        gain = parts[0:1] + parts[1:2] + parts[2:3]
                    tok[pipe if k == 0 else 1 - pipe] += (
                        parts[:, 0:128] + parts[:, 128:256] + parts[:, 256:384]
                    )
                scaled.append((rows * gain).astype(BF))
                rows = rows * rows
                for j in range(width // 128):
                    squares = squares + rows[:, j * 128 : (j + 1) * 128]
                weights.append(pl.ds(pl.multiple_of(t * width, 128), width))
            left = jnp.concatenate(scaled, axis=1)
            gate_w = jnp.concatenate([wg[rows, :] for rows in weights], axis=0)
            up_w = jnp.concatenate([wu[rows, :] for rows in weights], axis=0)
            gate = jnp.dot(left, gate_w, preferred_element_type=F32)
            up = jnp.dot(left, up_w, preferred_element_type=F32)
            for part, at in enumerate((pipe, 1 - pipe)):
                here = slice(part * 2 * half, (part + 1) * 2 * half)
                acc[at, :, 0:columns] += gate[here]
                acc[at, :, columns:] += up[here]
                ssq[at] += squares[here]
    sums[...] = tok[scal[2]]
    for pipe in range(2):
        total = jnp.sum(ssq[pipe], axis=1, keepdims=True)
        inverse = lax.rsqrt(total / (width * N_TENSOR) + NORM_EPS)
        keep = inverse > 0.0
        gate = jnp.where(keep, acc[pipe, :, 0:columns] * inverse, 0.0)
        up = jnp.where(keep, acc[pipe, :, columns:] * inverse, 0.0)
        hidden[pipe] = (gate * sigmoid(gate) * up).astype(BF)


IN_VMEM = pl.BlockSpec(memory_space=pltpu.VMEM)
IN_SMEM = pl.BlockSpec(memory_space=pltpu.SMEM)


def params(mib):
    return pltpu.CompilerParams(vmem_limit_bytes=mib * 1024 * 1024)


def gate_up(scal, near, far, wg, wu):
    rows = near[4].shape[1] * 2
    columns = wg.shape[1]
    return pl.pallas_call(
        gate_up_kernel,
        out_shape=[
            jax.ShapeDtypeStruct((2, rows, columns), BF),
            jax.ShapeDtypeStruct((16, 128), F32),
        ],
        in_specs=[IN_SMEM] + [IN_VMEM] * 18,
        out_specs=[IN_VMEM] * 2,
        scratch_shapes=[
            pltpu.VMEM((2, rows, 2 * columns), F32),
            pltpu.VMEM((2, rows, 128), F32),
            pltpu.VMEM((2, 16, 128), F32),
        ],
        compiler_params=params(28),
        name="gate_up",
    )(scal, *near, *far, wg, wu)


LATER = {0: 0, 1: 4, 3: 8}
FIRST_PIECES = {(2, 2): (True, True)}
LATER_PIECES = {}
for _j in (0, 1, 3):
    FIRST_PIECES[(2, _j)] = (True, False)
    FIRST_PIECES[(_j, 2)] = (False, True)
for _dy in (1, 3, 0, 2):
    for _dx in (1, 3, 0, 2):
        if _dy != 2 or _dx != 2:
            LATER_PIECES[(_dy, _dx)] = (_dy != 2, _dx != 2)


def down_products(scal, dc, hidden, wd, wanted):
    half = hidden.shape[1] // 2
    width = wd.shape[1] // N_TENSOR
    for (dy, dx), (with_a, with_b) in wanted.items():
        pipe, t = plane_target(scal, dc, dy, dx)
        if with_a and with_b:
            left = hidden[pipe]
        elif with_a:
            left = hidden[pipe, 0:half]
        else:
            left = hidden[pipe, half:]
        cols = pl.ds(pl.multiple_of(t * width, 128), width)
        out = jnp.dot(left, wd[:, cols], preferred_element_type=F32)
        a = out[0:half] if with_a else None
        b = (out[half:] if with_a else out) if with_b else None
        yield dy, dx, a, b


def far_first_kernel(scal, hidden, wd, out):
    for dy, dx, a, b in down_products(scal, 1, hidden, wd, FIRST_PIECES):
        if a is not None:
            out[dx] = a.astype(BF)
        if b is not None:
            out[4 + dy] = b.astype(BF)


def far_later_kernel(scal, hidden, wd, out):
    for dy, dx, a, b in down_products(scal, 1, hidden, wd, LATER_PIECES):
        if a is not None:
            out[LATER[dy] + dx] = a.astype(BF)
        if b is not None:
            out[12 + LATER[dx] + dy] = b.astype(BF)


def near_first_kernel(scal, hidden, wd, got, a2, b2):
    for dy, dx, a, b in down_products(scal, 0, hidden, wd, FIRST_PIECES):
        if a is not None:
            a2[dx] = (a + got[dx].astype(F32)).astype(BF)
        if b is not None:
            b2[dy] = (b + got[4 + dy].astype(F32)).astype(BF)


def near_later_kernel(scal, hidden, wd, got, a1, a3, a0, b1, b3, b0):
    a_out = {0: a0, 1: a1, 3: a3}
    b_out = {0: b0, 1: b1, 3: b3}
    for dy, dx, a, b in down_products(scal, 0, hidden, wd, LATER_PIECES):
        if a is not None:
            a_out[dy][dx] = (a + got[LATER[dy] + dx].astype(F32)).astype(BF)
        if b is not None:
            b_out[dx][dy] = (b + got[12 + LATER[dx] + dy].astype(F32)).astype(BF)


def down_call(kernel, counts, scal, hidden, wd, *got):
    half = hidden.shape[1] // 2
    width = wd.shape[1] // N_TENSOR
    return pl.pallas_call(
        kernel,
        out_shape=[jax.ShapeDtypeStruct((n, half, width), BF) for n in counts],
        in_specs=[IN_SMEM] + [IN_VMEM] * (2 + len(got)),
        out_specs=[IN_VMEM] * len(counts),
        compiler_params=params(20),
        name=kernel.__name__,
    )(scal, hidden, wd, *got)


def add(base, *parts):
    total = base.astype(F32)
    for part in parts:
        total = total + part.astype(F32)
    return total.astype(BF)


def expert_layer(scal, extra_rows, arrived, wg, wu, wd):
    together = lax.optimization_barrier
    half = arrived.shape[0] // 2
    top, low = jnp.concatenate([arrived[:half], extra_rows]), arrived[half:]
    x1, x3, y1, y3 = together(
        (from_x(top, 1), from_x(top, 3), from_plane(low, 0, 1), from_plane(low, 0, 3))
    )
    x2, y2 = together((from_x(x1, 1), from_plane(y1, 0, 1)))
    xa, yb = jnp.stack([top, x1, x2, x3]), jnp.stack([low, y1, y2, y3])
    xa, yb = together((xa, yb))
    au, ad, bu, bd = together(
        (from_plane(xa, 0, 1), from_plane(xa, 0, 3), from_x(yb, 1), from_x(yb, 3))
    )
    a2, b2 = from_plane(au, 0, 1), from_x(bu, 1)
    near = [xa, au, a2, ad, yb, bu, b2, bd]
    far = [from_flip(v, 1) for v in near]
    hidden, sums = gate_up(scal, near, far, wg, wu)

    (first,) = down_call(far_first_kernel, (8,), scal, hidden, wd)
    hidden, first = together((hidden, first))
    got_first = from_flip(first, 1)
    (later,) = down_call(far_later_kernel, (24,), scal, hidden, wd)
    got_later = from_flip(later, 1)
    a2, b2 = down_call(near_first_kernel, (4, 4), scal, hidden, wd, got_first)
    hidden, a2, b2 = together((hidden, a2, b2))
    ra2, rb2 = from_plane(a2, 0, 3), from_x(b2, 3)
    a1, a3, a0, b1, b3, b0 = down_call(near_later_kernel, (4,) * 6, scal, hidden, wd, got_later)
    ra2, rb2, ra3, rb3 = together((ra2, rb2, from_plane(a3, 0, 1), from_x(b3, 1)))
    ra1, rb1 = together((from_plane(add(a1, ra2), 0, 3), from_x(add(b1, rb2), 3)))
    a, b = add(a0, ra1, ra3), add(b0, rb1, rb3)
    ra2, rb2, ra3, rb3 = together(
        (from_x(a[2], 3), from_plane(b[2], 0, 3), from_x(a[3], 1), from_plane(b[3], 0, 1))
    )
    ra1, rb1 = from_x(add(a[1], ra2), 3), from_plane(add(b[1], rb2), 0, 3)
    return jnp.concatenate([add(a[0], ra1, ra3), add(b[0], rb1, rb3)]), sums


CORE_GROUPS = [list(range(0, 16, 2)), list(range(1, 16, 2))]


def exchange(value):
    return lax.all_to_all(
        value, "tensor", split_axis=0, concat_axis=0, axis_index_groups=CORE_GROUPS
    )


def product_blocks(scal, core, xt, wbuf):
    rows = xt.shape[1]
    for group in range(2):
        slots = []
        for j in range(group * 4, group * 4 + 4):
            t = j * 2 + core
            dp = lax.bitwise_xor(lax.shift_right_logical(t, 3), scal[2])
            dz = lax.bitwise_and(lax.bitwise_and(t, 7) - scal[3] + 8, 7)
            slots.append(dp * 8 + dz)
        left = jnp.concatenate([xt[slot] for slot in slots], axis=0)
        product = jnp.dot(left, wbuf[...], preferred_element_type=F32)
        for k, slot in enumerate(slots):
            yield group * 4 + k, slot, product[k * rows : (k + 1) * rows]


def store_block(out, j, product, squares):
    rows = product.shape[0]
    out[j, 0:rows] = product.astype(BF)
    high = squares.astype(BF)
    rest = squares - high.astype(F32)
    middle = rest.astype(BF)
    low = (rest - middle.astype(F32)).astype(BF)
    empty = jnp.zeros((16, product.shape[1] - 3 * rows), BF)
    wide = [jnp.broadcast_to(v.astype(F32), (16, rows)).astype(BF) for v in (high, middle, low)]
    out[j, rows : rows + 16] = jnp.concatenate(wide + [empty], axis=1)


def proj_far_kernel(scal, gain, *refs):
    n0, u1, d1, u2, d2, u3, d3, h4, l4, s1, s2 = refs[:11]
    wq, wk, wv, out, xt, sq, wbuf = refs[11:]
    half = h4.shape[0]
    n4 = jnp.concatenate([h4[...], l4[...]], axis=0)
    pieces = {0: n0, 1: u1, 7: d1, 2: u2, 6: d2, 3: u3, 5: d3}
    pieces = {i: ref[...] for i, ref in pieces.items()}
    pieces.update({4: n4, 8: s1[0], 9: s1[1], 15: s1[2], 10: s1[3], 14: s1[4]})
    pieces.update({11: s2[0], 13: s2[1], 12: s2[2]})
    ones = jnp.ones((8, n0.shape[1]), BF)
    over_features = functools.partial(
        lax.dot_general,
        dimension_numbers=(((1,), (1,)), ((), ())),
        preferred_element_type=F32,
    )
    for i, value in pieces.items():
        rows = value.astype(F32)
        xt[i] = (rows * gain[...]).astype(BF)
        squares = rows * rows
        high = squares.astype(BF)
        low = (squares - high.astype(F32)).astype(BF)
        sq[i] = over_features(ones, high) + over_features(ones, low)
    qw = wq.shape[1]
    head = pl.ds(pl.multiple_of(scal[4] * HD, HD), HD)
    wbuf[:, 0:qw] = wq[...]
    wbuf[:, qw : qw + HD] = wk[:, head]
    wbuf[:, qw + HD :] = wv[:, head]
    core = 1 - lax.bitwise_and(scal[0], 1)
    for j, slot, product in product_blocks(scal, core, xt, wbuf):
        store_block(out, j, product, sq[slot][0:1])


def proj_near_kernel(scal, got, xt, sq, wbuf, out):
    rows = xt.shape[1]
    core = lax.bitwise_and(scal[0], 1)
    for j, slot, product in product_blocks(scal, core, xt, wbuf):
        parts = got[j, rows : rows + 16].astype(F32)
        squares = sq[slot][0:1]
        for k in (2, 1, 0):
            squares = squares + parts[0:1, k * rows : (k + 1) * rows]
        store_block(out, j, product + got[j, 0:rows].astype(F32), squares)


def projections(scal, gain, tokens, wq, wk, wv):
    rows, width = tokens[0].shape
    columns = wq.shape[1] + 2 * HD
    sums = jax.ShapeDtypeStruct((8, rows + 16, columns), BF)
    far, xt, sq, wbuf = pl.pallas_call(
        proj_far_kernel,
        out_shape=[
            sums,
            jax.ShapeDtypeStruct((16, rows, width), BF),
            jax.ShapeDtypeStruct((16, 8, rows), F32),
            jax.ShapeDtypeStruct((width, columns), BF),
        ],
        in_specs=[IN_SMEM] + [IN_VMEM] * 15,
        out_specs=[IN_VMEM] * 4,
        compiler_params=params(20),
        name="proj_far",
    )(scal, gain, *tokens, wq, wk, wv)
    got = from_flip(far, 1)
    near = pl.pallas_call(
        proj_near_kernel,
        out_shape=sums,
        in_specs=[IN_SMEM] + [IN_VMEM] * 4,
        out_specs=IN_VMEM,
        compiler_params=params(20),
        name="proj_near",
    )(scal, got, xt, sq, wbuf)
    total = jnp.sum(exchange(near).astype(F32), axis=0)
    parts = total[rows, : 3 * rows].reshape(3, rows)
    return total[:rows], parts[0] + (parts[1] + parts[2])


def attend_kernel(scal, q, kv0, kv1, out):
    rows = q.shape[0]
    heads = q.shape[1] // HD
    own = scal[0]
    core = lax.bitwise_and(own, 1)
    keys, values, places = [], [], []
    for dc, kv in enumerate((kv0, kv1)):
        for j in range(8):
            block = kv[j]
            keys.append(block[:, :HD])
            values.append(block[:, HD:])
            base = (2 * j + lax.bitwise_xor(core, dc)) * rows
            places.append(lax.broadcasted_iota(jnp.int32, (rows, rows), 1) + base)
    keys = jnp.concatenate(keys, axis=0)
    values = jnp.concatenate(values, axis=0)
    places = jnp.concatenate(places, axis=1)
    mine = lax.broadcasted_iota(jnp.int32, places.shape, 0) + own * rows
    allowed = places <= mine
    for h in range(heads):
        scores = lax.dot_general(
            q[:, h * HD : (h + 1) * HD],
            keys,
            (((1,), (1,)), ((), ())),
            preferred_element_type=F32,
        ) * (1.0 / math.sqrt(HD))
        scores = jnp.where(allowed, scores, -1e30)
        best = jnp.max(scores, axis=1, keepdims=True)
        weights = jnp.where(allowed, jnp.exp(scores - best), 0.0)
        total = jnp.sum(weights, axis=1, keepdims=True)
        mixed = jnp.dot(weights.astype(BF), values, preferred_element_type=F32)
        out[:, h * HD : (h + 1) * HD] = (mixed / total).astype(BF)


def attend(scal, q, kv0, kv1):
    return pl.pallas_call(
        attend_kernel,
        out_shape=jax.ShapeDtypeStruct(q.shape, BF),
        in_specs=[IN_SMEM] + [IN_VMEM] * 3,
        out_specs=IN_VMEM,
        compiler_params=params(24),
        name="attend",
    )(scal, q, kv0, kv1)


def gather_tokens(own):
    half = own.shape[0] // 2
    u1, d1 = from_z(own, 1), from_z(own, 7)
    u2, d2 = from_z(u1, 1), from_z(d1, 7)
    s1 = from_pipe(jnp.stack([own, u1, d1, u2, d2]))
    u3, d3 = from_z(u2, 1), from_z(d2, 7)
    h4, l4 = from_z(u3[:half], 1), from_z(d3[half:], 7)
    s2 = from_pipe(jnp.stack([u3, d3, jnp.concatenate([h4, l4])]))
    return (own, u1, d1, u2, d2, u3, d3, h4, l4, s1, s2)


def on_device(
    stream,
    norm_gain,
    attn_gain,
    router,
    expert_ids,
    expert_slots,
    w_gate,
    w_up,
    w_down,
    w_query,
    w_key,
    w_value,
):
    token_rows, width = stream.shape
    features = width * N_TENSOR
    experts = router.shape[1]
    query_width = w_query.shape[1]
    heads_here = query_width // HD
    t = lax.axis_index("tensor")
    pipe = lax.axis_index("pipe")
    z = lax.axis_index("expert")
    kv_head = (pipe * 8 + z) * heads_here // (QH // KVH)
    yy = pipe * 2 + (t // 2) % 2
    scal = jnp.stack([t, yy, pipe, z, kv_head]).astype(jnp.int32)

    slot_total = experts * CAP
    target = jnp.where(expert_slots >= 0, expert_ids * CAP + expert_slots, slot_total)
    slots = jnp.arange(slot_total, dtype=jnp.int32)
    chosen = (slots[:, None] == target[:, 0][None]) | (slots[:, None] == target[:, 1][None])
    outgoing = jnp.dot(chosen.astype(BF), stream, preferred_element_type=F32).astype(BF)
    arrived = lax.all_to_all(outgoing, "expert", split_axis=0, concat_axis=0, tiled=True)

    stream_f = stream.astype(F32)
    logit_part = lax.dot_general(
        router, stream_f * norm_gain, (((0,), (1,)), ((), ())), precision=lax.Precision.HIGHEST
    )
    numbers = jnp.arange(experts, dtype=jnp.int32)[:, None]
    first_one = (numbers == expert_ids[:, 0][None]).astype(F32)
    second_one = (numbers == expert_ids[:, 1][None]).astype(F32)
    apart_part = jnp.sum(jnp.where(first_one > 0.0, logit_part, 0.0), axis=0) - jnp.sum(
        jnp.where(second_one > 0.0, logit_part, 0.0), axis=0
    )
    square_part = jnp.sum(stream_f * stream_f, axis=1)

    extra = jnp.stack([*split3(norm_gain)] + [jnp.concatenate(split3(v)) for v in (square_part, apart_part)])
    extra = jnp.concatenate([extra, jnp.zeros((11, width), BF)])
    expert_out, sums = expert_layer(scal, extra, arrived, w_gate[0], w_up[0], w_down[0])
    returned = lax.all_to_all(expert_out, "expert", split_axis=0, concat_axis=0, tiled=True)

    inverse = lax.rsqrt(sums[3] / features + NORM_EPS)
    first_share = jax.nn.sigmoid(inverse * sums[4])
    second_share = 1.0 - first_share

    wanted = jnp.concatenate([target[:, 0], target[:, 1]])
    picks = (wanted[:, None] == slots[None]).astype(BF)
    picked = jnp.dot(picks, returned, preferred_element_type=F32)
    moe_sum = (
        first_share[:, None] * picked[:token_rows] + second_share[:, None] * picked[token_rows:]
    )
    new_stream = (stream_f + moe_sum).astype(BF)

    tokens = gather_tokens(new_stream)
    own_proj, squares_two = projections(
        scal, attn_gain.reshape(1, width), tokens, w_query, w_key, w_value
    )
    inverse_two = lax.rsqrt(squares_two / features + NORM_EPS)[:, None]
    own_proj = jnp.where(inverse_two > 0.0, own_proj * inverse_two, 0.0).astype(BF)
    queries = own_proj[:, :query_width]
    kv = own_proj[:, query_width:]
    kv = exchange(jnp.broadcast_to(kv[None], (8,) + kv.shape))
    attended = attend(scal, queries, kv, from_flip(kv, 1))
    return (new_stream, attended)


def solution(mesh):
    in_specs = (
        P(("pipe", "expert"), "tensor"),
        P("tensor"),
        P("tensor"),
        P("tensor", None),
        P(("pipe", "expert"), None),
        P(("pipe", "expert"), None),
        P("expert", None, ("pipe", "tensor")),
        P("expert", None, ("pipe", "tensor")),
        P("expert", ("pipe", "tensor"), None),
        P("tensor", ("pipe", "expert")),
        P("tensor", None),
        P("tensor", None),
    )
    out_specs = (P(("pipe", "expert"), "tensor"), P("tensor", ("pipe", "expert")))
    return jax.shard_map(
        on_device, mesh=mesh, in_specs=in_specs, out_specs=out_specs, check_vma=False
    )
```

```python
import functools
import math

import jax
import jax.numpy as jnp
from jax import lax
from jax.experimental import pallas as pl
from jax.experimental.pallas import tpu as pltpu
from jax.sharding import PartitionSpec as P

HD = 128
QH = 48
KVH = 8
CAP = 40
NORM_EPS = 1e-05
N_TENSOR = 16
BF = jnp.bfloat16
F32 = jnp.float32


def from_axis(value, first, d):
    pairs = []
    for x in range(4):
        for yy in range(4):
            for core in range(2):
                along_x = (core == 0) == first
                tx = (x - d) % 4 if along_x else x
                ty = yy if along_x else (yy - d) % 4
                source = (yy // 2) * 16 + x * 4 + (yy % 2) * 2 + core
                pairs.append((source, (ty // 2) * 16 + tx * 4 + (ty % 2) * 2 + core))
    return lax.ppermute(value, ("pipe", "tensor"), pairs)


def from_flip(value, bit):
    return lax.ppermute(value, "tensor", [(i, i ^ bit) for i in range(16)])


def from_z(value, dz):
    return lax.ppermute(value, "expert", [(i, (i - dz) % 8) for i in range(8)])


def from_pipe(value):
    return lax.ppermute(value, "pipe", [(0, 1), (1, 0)])


def plane_target(scal, dy, dx):
    tx = lax.bitwise_and(lax.shift_right_logical(scal[0], 2) + dx, 3)
    ty = lax.bitwise_and(scal[1] + dy, 3)
    return lax.shift_right_logical(ty, 1), tx * 2 + lax.bitwise_and(ty, 1)


def sigmoid(v):
    return 1.0 / (1.0 + jnp.exp(-v))


IN_VMEM = pl.BlockSpec(memory_space=pltpu.VMEM)
IN_HBM = pl.BlockSpec(memory_space=pltpu.HBM)
IN_SMEM = pl.BlockSpec(memory_space=pltpu.SMEM)


def params(mib):
    return pltpu.CompilerParams(vmem_limit_bytes=mib * 1024 * 1024)


def prepare_kernel(*refs):
    outgoing, extra = refs[5:7]
    stream, gain, router, ids, slots = refs[7:12]
    copies = [pltpu.make_async_copy(refs[i], refs[7 + i], refs[12].at[i]) for i in range(5)]
    for copy in copies:
        copy.start()
    for copy in copies:
        copy.wait()
    experts = router.shape[0]
    tokens, width = stream.shape
    wanted = jnp.where(slots[...] >= 0, ids[...] * CAP + slots[...], experts * CAP)
    slot = lax.broadcasted_iota(jnp.int32, (experts * CAP, tokens), 0)
    chosen = (slot == wanted[0:1]) | (slot == wanted[1:2])
    chosen = jnp.where(chosen, 1.0, 0.0).astype(BF)
    rows = stream[...]
    outgoing[...] = jnp.dot(chosen, rows, preferred_element_type=F32).astype(BF)
    rows = rows.astype(F32)
    over_features = functools.partial(
        lax.dot_general,
        dimension_numbers=(((1,), (1,)), ((), ())),
        preferred_element_type=F32,
    )
    squares = rows * rows
    high = squares.astype(BF)
    low = (squares - high.astype(F32)).astype(BF)
    ones = jnp.ones((8, width), BF)
    square_sums = (over_features(ones, high) + over_features(ones, low))[0:1]
    logits = over_features(router[...], rows * gain[...], precision=lax.Precision.HIGHEST)
    number = lax.broadcasted_iota(jnp.int32, (experts, tokens), 0)
    apart = jnp.sum(jnp.where(number == ids[0:1], logits, 0.0), axis=0, keepdims=True) - jnp.sum(
        jnp.where(number == ids[1:2], logits, 0.0), axis=0, keepdims=True
    )

    def split(value):
        first = value.astype(BF).astype(F32)
        rest = value - first
        second = rest.astype(BF).astype(F32)
        return first, second, (rest - second).astype(BF).astype(F32)

    lines = list(split(gain[...]))
    empty = [jnp.zeros((1, width - 3 * tokens), F32)] if width > 3 * tokens else []
    lines += [jnp.concatenate(list(split(v)) + empty, axis=1) for v in (square_sums, apart)]
    line = lax.broadcasted_iota(jnp.int32, (16, width), 0)
    out = jnp.zeros((16, width), F32)
    for i, value in enumerate(lines):
        out = jnp.where(line == i, value, out)
    extra[...] = out.astype(BF)


def prepare(stream, gain, router, ids, slots):
    experts = router.shape[0]
    width = stream.shape[1]
    return pl.pallas_call(
        prepare_kernel,
        out_shape=[
            jax.ShapeDtypeStruct((experts * CAP, width), BF),
            jax.ShapeDtypeStruct((16, width), BF),
        ],
        in_specs=[IN_HBM] * 5,
        out_specs=[IN_VMEM] * 2,
        scratch_shapes=[pltpu.VMEM(v.shape, v.dtype) for v in (stream, gain, router, ids, slots)]
        + [pltpu.SemaphoreType.DMA((5,))],
        compiler_params=params(8),
        name="prepare",
    )(stream, gain, router, ids, slots)


def halves_kernel(scal, arrived, extra, keep, send):
    core = lax.bitwise_and(scal[0], 1)
    half = arrived.shape[0] // 2
    for out, which in ((keep, core), (send, 1 - core)):
        out[0:half] = arrived[pl.ds(pl.multiple_of(which * half, 16), half), :]
        out[half : half + 16] = extra[...]


def pair_kernel(scal, own, got, out):
    core = lax.bitwise_and(scal[0], 1)
    out[core] = own[...]
    out[1 - core] = got[...]


def stack_kernel(v0, v1, v2, v3, low, high):
    low[0] = v0[...]
    low[1] = v1[...]
    high[0] = v2[...]
    high[1] = v3[...]


def small_call(kernel, shapes, scal, *values):
    specs = [IN_VMEM] * len(values)
    if scal is not None:
        specs, values = [IN_SMEM] + specs, (scal,) + values
    return pl.pallas_call(
        kernel,
        out_shape=[jax.ShapeDtypeStruct(shape, BF) for shape in shapes],
        in_specs=specs,
        out_specs=[IN_VMEM] * len(shapes),
        compiler_params=params(8),
        name=kernel.__name__,
    )(*values)


def accumulate(scal, piece, steps, wg, wu, acc, ssq):
    columns = wg.shape[1]
    half = acc.shape[1]
    for (parity, dx), segments in steps.items():
        _, pair = plane_target(scal, parity, dx)
        scaled = []
        squares = 0.0
        for core in range(2):
            blocks = [piece(kind, dy, dx) for kind, dy in segments]
            blocks = [ref.at[index, core] for ref, index in blocks]
            parts = blocks[0][half : half + 16].astype(F32)
            gain = parts[0:1] + parts[1:2] + parts[2:3]
            rows = jnp.concatenate([block[0:half] for block in blocks], axis=0).astype(F32)
            width = rows.shape[1]
            scaled.append((rows * gain).astype(BF))
            rows = rows * rows
            for j in range(width // 128):
                squares = squares + rows[:, j * 128 : (j + 1) * 128]
        left = jnp.concatenate(scaled, axis=1)
        rows = pl.ds(pl.multiple_of(pair * 2 * width, 128), 2 * width)
        gate = jnp.dot(left, wg[rows, :], preferred_element_type=F32)
        up = jnp.dot(left, wu[rows, :], preferred_element_type=F32)
        for k, (kind, dy) in enumerate(segments):
            pipe, _ = plane_target(scal, dy, dx)
            to = pipe * 2 + (kind == "b")
            here = slice(k * half, (k + 1) * half)
            acc[to, :, 0:columns] += gate[here]
            acc[to, :, columns:] += up[here]
            ssq[to] += squares[here]


def token_sums(scal, refs, dy, tok, half):
    pipe, _ = plane_target(scal, dy, 0)
    for dx in range(4):
        for core in range(2):
            parts = refs[dx // 2][dx % 2, core, half : half + 16].astype(F32)
            tok[pipe] += parts[:, 0:128] + parts[:, 128:256] + parts[:, 256:384]


EARLY_STEPS = {}
LATE_STEPS = {(1, 2): (("b", 1), ("b", 3))}
for _dx in range(4):
    if _dx == 2:
        EARLY_STEPS[(0, 2)] = (("a", 0),)
        EARLY_STEPS[(1, 2)] = (("a", 1), ("a", 3))
        LATE_STEPS[(0, 2)] = (("b", 0), ("a", 2), ("b", 2))
    else:
        EARLY_STEPS[(0, _dx)] = (("a", 0), ("b", 0), ("b", 2))
        EARLY_STEPS[(1, _dx)] = (("a", 1), ("b", 1), ("a", 3), ("b", 3))
        LATE_STEPS[(0, _dx)] = (("a", 2),)


def on_each_core(scal, own, other, body):
    core = lax.bitwise_and(scal[0], 1)
    pl.when(core == 0)(lambda: body(own, other))
    pl.when(core == 1)(lambda: body(other, own))


def gate_up_early_kernel(scal, *refs):
    wg, wu, acc, ssq, tok = refs[12:]
    half = acc.shape[1]
    acc[...] = jnp.zeros_like(acc)
    ssq[...] = jnp.zeros_like(ssq)
    tok[...] = jnp.zeros_like(tok)

    def body(half_a, half_b):
        at = {0: 0, 1: 2, 3: 4}

        def piece(kind, dy, dx):
            first, second, refs = (dx, dy, half_a) if kind == "a" else (dy, dx, half_b)
            return refs[at[second] + first // 2], first % 2

        accumulate(scal, piece, EARLY_STEPS, wg, wu, acc, ssq)
        for dy in (0, 1, 3):
            token_sums(scal, half_a[at[dy] : at[dy] + 2], dy, tok, half)

    on_each_core(scal, refs[0:6], refs[6:12], body)


def gate_up_late_kernel(scal, *refs):
    wg, wu, acc_in, ssq_in, tok_in, hidden, sums, acc, ssq, tok = refs[4:]
    columns = wg.shape[1]
    acc[...] = acc_in[...]
    ssq[...] = ssq_in[...]
    tok[...] = tok_in[...]

    def body(half_a, half_b):
        def piece(kind, dy, dx):
            first, refs = (dx, half_a) if kind == "a" else (dy, half_b)
            return refs[first // 2], first % 2

        accumulate(scal, piece, LATE_STEPS, wg, wu, acc, ssq)
        token_sums(scal, half_a, 2, tok, acc.shape[1])

    on_each_core(scal, refs[0:2], refs[2:4], body)
    sums[...] = tok[scal[2]]
    features = wg.shape[0]
    for i in range(4):
        total = jnp.sum(ssq[i], axis=1, keepdims=True)
        inverse = lax.rsqrt(total / features + NORM_EPS)
        keep = inverse > 0.0
        gate = jnp.where(keep, acc[i, :, 0:columns] * inverse, 0.0)
        up = jnp.where(keep, acc[i, :, columns:] * inverse, 0.0)
        hidden[i] = (gate * sigmoid(gate) * up).astype(BF)


def gate_up_early(scal, own, other, wg, wu):
    half = own[0].shape[2] - 16
    return pl.pallas_call(
        gate_up_early_kernel,
        out_shape=[
            jax.ShapeDtypeStruct((4, half, 2 * wg.shape[1]), F32),
            jax.ShapeDtypeStruct((4, half, 128), F32),
            jax.ShapeDtypeStruct((2, 16, 128), F32),
        ],
        in_specs=[IN_SMEM] + [IN_VMEM] * 14,
        out_specs=[IN_VMEM] * 3,
        compiler_params=params(28),
        name="gate_up_early",
    )(scal, *own, *other, wg, wu)


def gate_up_late(scal, own, other, wg, wu, acc, ssq, tok):
    return pl.pallas_call(
        gate_up_late_kernel,
        out_shape=[
            jax.ShapeDtypeStruct((4, acc.shape[1], wg.shape[1]), BF),
            jax.ShapeDtypeStruct((16, 128), F32),
        ],
        in_specs=[IN_SMEM] + [IN_VMEM] * 9,
        out_specs=[IN_VMEM] * 2,
        scratch_shapes=[pltpu.VMEM(v.shape, F32) for v in (acc, ssq, tok)],
        compiler_params=params(28),
        name="gate_up_late",
    )(scal, *own, *other, wg, wu, acc, ssq, tok)


def down_kernel(far, steps, scal, hidden, wd, out):
    core = lax.bitwise_and(scal[0], 1)
    if far:
        core = 1 - core
    width = out.shape[3]
    for i, second in enumerate(steps):
        for first in range(4):
            dx = first + core * (second - first)
            dy = second + core * (first - second)
            pipe, pair = plane_target(scal, dy, dx)
            cols = pl.ds(pl.multiple_of(pair * 2 * width, 128), 2 * width)
            product = jnp.dot(hidden[pipe * 2 + core], wd[:, cols], preferred_element_type=F32)
            out[4 * i + first, 0] = product[:, 0:width].astype(BF)
            out[4 * i + first, 1] = product[:, width:].astype(BF)


def down(far, steps, scal, hidden, wd):
    shape = (4 * len(steps), 2, hidden.shape[1], wd.shape[1] // N_TENSOR)
    return pl.pallas_call(
        functools.partial(down_kernel, far, steps),
        out_shape=jax.ShapeDtypeStruct(shape, BF),
        in_specs=[IN_SMEM] + [IN_VMEM] * 2,
        out_specs=IN_VMEM,
        compiler_params=params(20),
        name=f"down_{'far' if far else 'near'}_{len(steps)}",
    )(scal, hidden, wd)


def add(base, *parts):
    total = base.astype(F32)
    for part in parts:
        total = total + part.astype(F32)
    return total.astype(BF)


def expert_layer(scal, extra, arrived, wg, wu, wd):
    together = lax.optimization_barrier
    half, width = arrived.shape[0] // 2, arrived.shape[1]
    block = (half + 16, width)
    keep, send = small_call(halves_kernel, [block] * 2, scal, arrived, extra)
    (both,) = small_call(pair_kernel, [(2,) + block], scal, keep, from_flip(send, 1))
    lines = [both] + [from_axis(both, True, d) for d in (1, 2, 3)]
    low0, high0 = small_call(stack_kernel, [(2, 2) + block] * 2, None, *lines)
    low1, high3 = from_axis(low0, False, 1), from_axis(high0, False, 3)
    high1, low3 = from_axis(high0, False, 1), from_axis(low0, False, 3)
    low2, high2 = from_axis(low1, False, 1), from_axis(high3, False, 3)
    own = (low0, high0, low1, high1, low3, high3)
    sofar = gate_up_early(scal, own, [from_flip(v, 1) for v in own], wg, wu)
    low2, high2, sofar = together((low2, high2, sofar))
    other = (from_flip(low2, 1), from_flip(high2, 1))
    hidden, sums = gate_up_late(scal, (low2, high2), other, wg, wu, *sofar)

    far = down(True, (2,), scal, hidden, wd)
    hidden, far = together((hidden, far))
    got = from_flip(far, 1)
    own = down(False, (2,), scal, hidden, wd)
    low2, high2 = add(own[:2], got[:2]), add(own[2:], got[2:])
    hidden, low2, high2 = together((hidden, low2, high2))
    low2, high2 = from_axis(low2, False, 3), from_axis(high2, False, 1)
    far = down(True, (0, 1, 3), scal, hidden, wd)
    hidden, far = together((hidden, far))
    got = from_flip(far, 1)
    own = down(False, (0, 1, 3), scal, hidden, wd)
    low0, high0, low1, high1, low3, high3 = (
        (own[i : i + 2], got[i : i + 2]) for i in range(0, 12, 2)
    )
    high1, low3 = from_axis(add(*high1), False, 3), from_axis(add(*low3), False, 1)
    low1, high3 = from_axis(add(*low1, low2), False, 3), from_axis(add(*high3, high2), False, 1)
    low1, high3, high1, low3 = together((low1, high3, high1, low3))
    low0, high0 = add(*low0, low1, low3), add(*high0, high1, high3)
    line = (low0[0], low0[1], high0[0], high0[1])
    done = add(line[0], *(from_axis(line[d], True, 4 - d) for d in (1, 2, 3)))
    core = lax.bitwise_and(scal[0], 1)
    mine = lax.dynamic_index_in_dim(done, core, 0, keepdims=False)
    other = from_flip(lax.dynamic_index_in_dim(done, 1 - core, 0, keepdims=False), 1)
    first = core == 0
    rows = [jnp.where(first, mine, other), jnp.where(first, other, mine)]
    return jnp.concatenate(rows), sums


CORE_GROUPS = [list(range(0, 16, 2)), list(range(1, 16, 2))]


def exchange(value):
    return lax.all_to_all(
        value, "tensor", split_axis=0, concat_axis=0, axis_index_groups=CORE_GROUPS
    )


def product_blocks(scal, core, xt, wbuf):
    rows = xt.shape[1]
    for group in range(2):
        slots = []
        for j in range(group * 4, group * 4 + 4):
            t = j * 2 + core
            dp = lax.bitwise_xor(lax.shift_right_logical(t, 3), scal[2])
            dz = lax.bitwise_and(lax.bitwise_and(t, 7) - scal[3] + 8, 7)
            slots.append(dp * 8 + dz)
        left = jnp.concatenate([xt[slot] for slot in slots], axis=0)
        product = jnp.dot(left, wbuf[...], preferred_element_type=F32)
        for k, slot in enumerate(slots):
            yield group * 4 + k, slot, product[k * rows : (k + 1) * rows]


def store_block(out, j, product, squares):
    rows = product.shape[0]
    out[j, 0:rows] = product.astype(BF)
    high = squares.astype(BF)
    rest = squares - high.astype(F32)
    middle = rest.astype(BF)
    low = (rest - middle.astype(F32)).astype(BF)
    empty = jnp.zeros((16, product.shape[1] - 3 * rows), BF)
    wide = [jnp.broadcast_to(v.astype(F32), (16, rows)).astype(BF) for v in (high, middle, low)]
    out[j, rows : rows + 16] = jnp.concatenate(wide + [empty], axis=1)


def proj_far_kernel(scal, gain, *refs):
    n0, u1, d1, u2, d2, u3, d3, h4, l4, s1, s2, s3 = refs[:12]
    wq, wk, wv, out, xt, sq, wbuf = refs[12:]
    half = h4.shape[0]
    n4 = jnp.concatenate([h4[...], l4[...]], axis=0)
    pieces = {0: n0, 1: u1, 7: d1, 2: u2, 6: d2, 3: u3, 5: d3}
    pieces = {i: ref[...] for i, ref in pieces.items()}
    pieces.update({4: n4, 8: s1[0], 9: s1[1], 15: s1[2], 12: s3[...]})
    pieces.update({10: s2[0], 14: s2[1], 11: s2[2], 13: s2[3]})
    ones = jnp.ones((8, n0.shape[1]), BF)
    over_features = functools.partial(
        lax.dot_general,
        dimension_numbers=(((1,), (1,)), ((), ())),
        preferred_element_type=F32,
    )
    for i, value in pieces.items():
        rows = value.astype(F32)
        xt[i] = (rows * gain[...]).astype(BF)
        squares = rows * rows
        high = squares.astype(BF)
        low = (squares - high.astype(F32)).astype(BF)
        sq[i] = over_features(ones, high) + over_features(ones, low)
    qw = wq.shape[1]
    head = pl.ds(pl.multiple_of(scal[4] * HD, HD), HD)
    wbuf[:, 0:qw] = wq[...]
    wbuf[:, qw : qw + HD] = wk[:, head]
    wbuf[:, qw + HD :] = wv[:, head]
    core = 1 - lax.bitwise_and(scal[0], 1)
    for j, slot, product in product_blocks(scal, core, xt, wbuf):
        store_block(out, j, product, sq[slot][0:1])


def proj_near_kernel(scal, got, xt, sq, wbuf, out):
    rows = xt.shape[1]
    core = lax.bitwise_and(scal[0], 1)
    for j, slot, product in product_blocks(scal, core, xt, wbuf):
        parts = got[j, rows : rows + 16].astype(F32)
        squares = sq[slot][0:1]
        for k in (2, 1, 0):
            squares = squares + parts[0:1, k * rows : (k + 1) * rows]
        store_block(out, j, product + got[j, 0:rows].astype(F32), squares)


def projections(scal, gain, tokens, wq, wk, wv):
    rows, width = tokens[0].shape
    columns = wq.shape[1] + 2 * HD
    sums = jax.ShapeDtypeStruct((8, rows + 16, columns), BF)
    far, xt, sq, wbuf = pl.pallas_call(
        proj_far_kernel,
        out_shape=[
            sums,
            jax.ShapeDtypeStruct((16, rows, width), BF),
            jax.ShapeDtypeStruct((16, 8, rows), F32),
            jax.ShapeDtypeStruct((width, columns), BF),
        ],
        in_specs=[IN_SMEM] + [IN_VMEM] * 16,
        out_specs=[IN_VMEM] * 4,
        compiler_params=params(20),
        name="proj_far",
    )(scal, gain, *tokens, wq, wk, wv)
    got = from_flip(far, 1)
    near = pl.pallas_call(
        proj_near_kernel,
        out_shape=sums,
        in_specs=[IN_SMEM] + [IN_VMEM] * 4,
        out_specs=IN_VMEM,
        compiler_params=params(20),
        name="proj_near",
    )(scal, got, xt, sq, wbuf)
    total = jnp.sum(exchange(near).astype(F32), axis=0)
    parts = total[rows, : 3 * rows].reshape(3, rows)
    return total[:rows], parts[0] + (parts[1] + parts[2])


def attend_kernel(scal, q, kv0, kv1, out):
    rows = q.shape[0]
    heads = q.shape[1] // HD
    own = scal[0]
    core = lax.bitwise_and(own, 1)
    keys, values, places = [], [], []
    for dc, kv in enumerate((kv0, kv1)):
        for j in range(8):
            block = kv[j]
            keys.append(block[:, :HD])
            values.append(block[:, HD:])
            base = (2 * j + lax.bitwise_xor(core, dc)) * rows
            places.append(lax.broadcasted_iota(jnp.int32, (rows, rows), 1) + base)
    keys = jnp.concatenate(keys, axis=0)
    values = jnp.concatenate(values, axis=0)
    places = jnp.concatenate(places, axis=1)
    mine = lax.broadcasted_iota(jnp.int32, places.shape, 0) + own * rows
    allowed = places <= mine
    for h in range(heads):
        scores = lax.dot_general(
            q[:, h * HD : (h + 1) * HD],
            keys,
            (((1,), (1,)), ((), ())),
            preferred_element_type=F32,
        ) * (1.0 / math.sqrt(HD))
        scores = jnp.where(allowed, scores, -1e30)
        best = jnp.max(scores, axis=1, keepdims=True)
        weights = jnp.where(allowed, jnp.exp(scores - best), 0.0)
        total = jnp.sum(weights, axis=1, keepdims=True)
        mixed = jnp.dot(weights.astype(BF), values, preferred_element_type=F32)
        out[:, h * HD : (h + 1) * HD] = (mixed / total).astype(BF)


def attend(scal, q, kv0, kv1):
    return pl.pallas_call(
        attend_kernel,
        out_shape=jax.ShapeDtypeStruct(q.shape, BF),
        in_specs=[IN_SMEM] + [IN_VMEM] * 3,
        out_specs=IN_VMEM,
        compiler_params=params(24),
        name="attend",
    )(scal, q, kv0, kv1)


def gather_tokens(own):
    half = own.shape[0] // 2
    u1, d1 = from_z(own, 1), from_z(own, 7)
    s1 = from_pipe(jnp.stack([own, u1, d1]))
    u2, d2 = from_z(u1, 1), from_z(d1, 7)
    u3, d3 = from_z(u2, 1), from_z(d2, 7)
    s2 = from_pipe(jnp.stack([u2, d2, u3, d3]))
    h4, l4 = from_z(u3[:half], 1), from_z(d3[half:], 7)
    s3 = from_pipe(jnp.concatenate([h4, l4]))
    return (own, u1, d1, u2, d2, u3, d3, h4, l4, s1, s2, s3)


def on_device(
    stream,
    norm_gain,
    attn_gain,
    router,
    expert_ids,
    expert_slots,
    w_gate,
    w_up,
    w_down,
    w_query,
    w_key,
    w_value,
):
    token_rows, width = stream.shape
    features = width * N_TENSOR
    experts = router.shape[1]
    query_width = w_query.shape[1]
    heads_here = query_width // HD
    t = lax.axis_index("tensor")
    pipe = lax.axis_index("pipe")
    z = lax.axis_index("expert")
    kv_head = (pipe * 8 + z) * heads_here // (QH // KVH)
    yy = pipe * 2 + (t // 2) % 2
    scal = jnp.stack([t, yy, pipe, z, kv_head]).astype(jnp.int32)

    outgoing, extra = prepare(
        stream, norm_gain.reshape(1, width), router.T, expert_ids.T, expert_slots.T
    )
    scal, outgoing, extra = lax.optimization_barrier((scal, outgoing, extra))
    arrived = lax.all_to_all(outgoing, "expert", split_axis=0, concat_axis=0, tiled=True)
    expert_out, sums = expert_layer(scal, extra, arrived, w_gate[0], w_up[0], w_down[0])
    returned = lax.all_to_all(expert_out, "expert", split_axis=0, concat_axis=0, tiled=True)

    inverse = lax.rsqrt(sums[3] / features + NORM_EPS)
    first_share = jax.nn.sigmoid(inverse * sums[4])
    second_share = 1.0 - first_share

    slot_total = experts * CAP
    target = jnp.where(expert_slots >= 0, expert_ids * CAP + expert_slots, slot_total)
    slots = jnp.arange(slot_total, dtype=jnp.int32)
    stream_f = stream.astype(F32)
    wanted = jnp.concatenate([target[:, 0], target[:, 1]])
    picks = (wanted[:, None] == slots[None]).astype(BF)
    picked = jnp.dot(picks, returned, preferred_element_type=F32)
    moe_sum = (
        first_share[:, None] * picked[:token_rows] + second_share[:, None] * picked[token_rows:]
    )
    new_stream = (stream_f + moe_sum).astype(BF)

    tokens = gather_tokens(new_stream)
    own_proj, squares_two = projections(
        scal, attn_gain.reshape(1, width), tokens, w_query, w_key, w_value
    )
    inverse_two = lax.rsqrt(squares_two / features + NORM_EPS)[:, None]
    own_proj = jnp.where(inverse_two > 0.0, own_proj * inverse_two, 0.0).astype(BF)
    queries = own_proj[:, :query_width]
    kv = own_proj[:, query_width:]
    kv = exchange(jnp.broadcast_to(kv[None], (8,) + kv.shape))
    attended = attend(scal, queries, kv, from_flip(kv, 1))
    return (new_stream, attended)


def solution(mesh):
    in_specs = (
        P(("pipe", "expert"), "tensor"),
        P("tensor"),
        P("tensor"),
        P("tensor", None),
        P(("pipe", "expert"), None),
        P(("pipe", "expert"), None),
        P("expert", None, ("pipe", "tensor")),
        P("expert", None, ("pipe", "tensor")),
        P("expert", ("pipe", "tensor"), None),
        P("tensor", ("pipe", "expert")),
        P("tensor", None),
        P("tensor", None),
    )
    out_specs = (P(("pipe", "expert"), "tensor"), P("tensor", ("pipe", "expert")))
    return jax.shard_map(
        on_device, mesh=mesh, in_specs=in_specs, out_specs=out_specs, check_vma=False
    )
```

```python
import functools
import math

import jax
import jax.numpy as jnp
from jax import lax
from jax.experimental import pallas as pl
from jax.experimental.pallas import tpu as pltpu
from jax.sharding import PartitionSpec as P

HD = 128
QH = 48
KVH = 8
CAP = 40
NORM_EPS = 1e-05
N_TENSOR = 16
BF = jnp.bfloat16
F32 = jnp.float32


def from_axis(value, first, d):
    pairs = []
    for x in range(4):
        for yy in range(4):
            for core in range(2):
                along_x = (core == 0) == first
                tx = (x - d) % 4 if along_x else x
                ty = yy if along_x else (yy - d) % 4
                source = (yy // 2) * 16 + x * 4 + (yy % 2) * 2 + core
                pairs.append((source, (ty // 2) * 16 + tx * 4 + (ty % 2) * 2 + core))
    return lax.ppermute(value, ("pipe", "tensor"), pairs)


def from_flip(value, bit):
    return lax.ppermute(value, "tensor", [(i, i ^ bit) for i in range(16)])


def from_z(value, dz):
    return lax.ppermute(value, "expert", [(i, (i - dz) % 8) for i in range(8)])


def from_pipe(value):
    return lax.ppermute(value, "pipe", [(0, 1), (1, 0)])


def plane_target(scal, dy, dx):
    tx = lax.bitwise_and(lax.shift_right_logical(scal[0], 2) + dx, 3)
    ty = lax.bitwise_and(scal[1] + dy, 3)
    return lax.shift_right_logical(ty, 1), tx * 2 + lax.bitwise_and(ty, 1)


def sigmoid(v):
    return 1.0 / (1.0 + jnp.exp(-v))


IN_VMEM = pl.BlockSpec(memory_space=pltpu.VMEM)
IN_HBM = pl.BlockSpec(memory_space=pltpu.HBM)
IN_SMEM = pl.BlockSpec(memory_space=pltpu.SMEM)


def params(mib):
    return pltpu.CompilerParams(vmem_limit_bytes=mib * 1024 * 1024)


def prepare_kernel(*refs):
    outgoing, extra = refs[5:7]
    stream, gain, router, ids, slots = refs[7:12]
    copies = [pltpu.make_async_copy(refs[i], refs[7 + i], refs[12].at[i]) for i in range(5)]
    for copy in copies:
        copy.start()
    for copy in copies:
        copy.wait()
    experts = router.shape[0]
    tokens, width = stream.shape
    wanted = jnp.where(slots[...] >= 0, ids[...] * CAP + slots[...], experts * CAP)
    slot = lax.broadcasted_iota(jnp.int32, (experts * CAP, tokens), 0)
    chosen = (slot == wanted[0:1]) | (slot == wanted[1:2])
    chosen = jnp.where(chosen, 1.0, 0.0).astype(BF)
    rows = stream[...]
    outgoing[...] = jnp.dot(chosen, rows, preferred_element_type=F32).astype(BF)
    rows = rows.astype(F32)
    over_features = functools.partial(
        lax.dot_general,
        dimension_numbers=(((1,), (1,)), ((), ())),
        preferred_element_type=F32,
    )
    squares = rows * rows
    high = squares.astype(BF)
    low = (squares - high.astype(F32)).astype(BF)
    ones = jnp.ones((8, width), BF)
    square_sums = (over_features(ones, high) + over_features(ones, low))[0:1]
    logits = over_features(router[...], rows * gain[...], precision=lax.Precision.HIGHEST)
    number = lax.broadcasted_iota(jnp.int32, (experts, tokens), 0)
    apart = jnp.sum(jnp.where(number == ids[0:1], logits, 0.0), axis=0, keepdims=True) - jnp.sum(
        jnp.where(number == ids[1:2], logits, 0.0), axis=0, keepdims=True
    )

    def split(value):
        first = value.astype(BF).astype(F32)
        rest = value - first
        second = rest.astype(BF).astype(F32)
        return first, second, (rest - second).astype(BF).astype(F32)

    lines = list(split(gain[...]))
    empty = [jnp.zeros((1, width - 3 * tokens), F32)] if width > 3 * tokens else []
    lines += [jnp.concatenate(list(split(v)) + empty, axis=1) for v in (square_sums, apart)]
    line = lax.broadcasted_iota(jnp.int32, (16, width), 0)
    out = jnp.zeros((16, width), F32)
    for i, value in enumerate(lines):
        out = jnp.where(line == i, value, out)
    extra[...] = out.astype(BF)


def prepare(stream, gain, router, ids, slots):
    experts = router.shape[0]
    width = stream.shape[1]
    return pl.pallas_call(
        prepare_kernel,
        out_shape=[
            jax.ShapeDtypeStruct((experts * CAP, width), BF),
            jax.ShapeDtypeStruct((16, width), BF),
        ],
        in_specs=[IN_HBM] * 5,
        out_specs=[IN_VMEM] * 2,
        scratch_shapes=[pltpu.VMEM(v.shape, v.dtype) for v in (stream, gain, router, ids, slots)]
        + [pltpu.SemaphoreType.DMA((5,))],
        compiler_params=params(8),
        name="prepare",
    )(stream, gain, router, ids, slots)


def halves_kernel(scal, arrived, extra, keep, send):
    core = lax.bitwise_and(scal[0], 1)
    half = arrived.shape[0] // 2
    blocks = arrived.shape[0] // CAP
    rows = arrived[...].astype(F32)
    rows = [rows[j * CAP : (j + 1) * CAP] for j in reversed(range(blocks))]
    first = jnp.concatenate(rows[: blocks // 2], axis=0).astype(BF)
    second = jnp.concatenate(rows[blocks // 2 :], axis=0).astype(BF)
    keep[0:half] = jnp.where(core == 0, first, second)
    send[0:half] = jnp.where(core == 0, second, first)
    keep[half : half + 16] = extra[...]
    send[half : half + 16] = extra[...]


def pair_kernel(scal, own, got, out):
    core = lax.bitwise_and(scal[0], 1)
    out[core] = own[...]
    out[1 - core] = got[...]


def stack_kernel(v0, v1, v2, v3, low, high):
    low[0] = v0[...]
    low[1] = v1[...]
    high[0] = v2[...]
    high[1] = v3[...]


def join_kernel(v0, v1, v2, v3, up, down):
    up[0:2] = v0[...]
    up[2:4] = v1[...]
    down[0:2] = v2[...]
    down[2:4] = v3[...]


def small_call(kernel, shapes, scal, *values):
    specs = [IN_VMEM] * len(values)
    if scal is not None:
        specs, values = [IN_SMEM] + specs, (scal,) + values
    return pl.pallas_call(
        kernel,
        out_shape=[jax.ShapeDtypeStruct(shape, BF) for shape in shapes],
        in_specs=specs,
        out_specs=[IN_VMEM] * len(shapes),
        compiler_params=params(8),
        name=kernel.__name__,
    )(*values)


def accumulate(scal, piece, steps, wg, wu, acc, ssq):
    columns = wg.shape[1]
    half = acc.shape[1]
    for (parity, dx), segments in steps.items():
        _, pair = plane_target(scal, parity, dx)
        scaled = []
        squares = 0.0
        for core in range(2):
            blocks = [piece(kind, dy, dx) for kind, dy in segments]
            blocks = [ref.at[index, core] for ref, index in blocks]
            parts = blocks[0][half : half + 16].astype(F32)
            gain = parts[0:1] + parts[1:2] + parts[2:3]
            rows = jnp.concatenate([block[0:half] for block in blocks], axis=0).astype(F32)
            width = rows.shape[1]
            scaled.append((rows * gain).astype(BF))
            rows = rows * rows
            for j in range(width // 128):
                squares = squares + rows[:, j * 128 : (j + 1) * 128]
        left = jnp.concatenate(scaled, axis=1)
        rows = pl.ds(pl.multiple_of(pair * 2 * width, 128), 2 * width)
        gate = jnp.dot(left, wg[rows, :], preferred_element_type=F32)
        up = jnp.dot(left, wu[rows, :], preferred_element_type=F32)
        for k, (kind, dy) in enumerate(segments):
            pipe, _ = plane_target(scal, dy, dx)
            to = pipe * 2 + (kind == "b")
            here = slice(k * half, (k + 1) * half)
            acc[to, :, 0:columns] += gate[here]
            acc[to, :, columns:] += up[here]
            ssq[to] += squares[here]


def steps_of(blocks):
    steps = {}
    for parity in range(2):
        for dx in range(4):
            segments = []
            for dy in (parity, parity + 2):
                segments += [("a", dy)] if (dy, dx // 2) in blocks else []
                segments += [("b", dy)] if (dx, dy // 2) in blocks else []
            if segments:
                steps[(parity, dx)] = segments
    return steps


def on_each_core(scal, own, other, body):
    core = lax.bitwise_and(scal[0], 1)
    pl.when(core == 0)(lambda: body(own, other))
    pl.when(core == 1)(lambda: body(other, own))


def gate_up_kernel(blocks, count, started, last, scal, *refs):
    own, other = refs[:count], refs[count : 2 * count]
    wg, wu = refs[2 * count : 2 * count + 2]
    refs = refs[2 * count + 2 :]
    acc, ssq, tok = refs[-3:]
    half = acc.shape[1]
    if started:
        for ref, before in zip((acc, ssq, tok), refs):
            ref[...] = before[...]
    else:
        for ref in (acc, ssq, tok):
            ref[...] = jnp.zeros_like(ref)

    def body(half_a, half_b):
        def piece(kind, dy, dx):
            first, second, table = (dx, dy, half_a) if kind == "a" else (dy, dx, half_b)
            array, start = blocks[(second, first // 2)]
            return table[array], start + first % 2

        accumulate(scal, piece, steps_of(blocks), wg, wu, acc, ssq)
        for (dy, _), (array, start) in blocks.items():
            pipe, _ = plane_target(scal, dy, 0)
            for at in (start, start + 1):
                for core in range(2):
                    parts = half_a[array][at, core, half : half + 16].astype(F32)
                    tok[pipe] += parts[:, 0:128] + parts[:, 128:256] + parts[:, 256:384]

    on_each_core(scal, own, other, body)
    if not last:
        return
    hidden, sums = refs[3:5]
    sums[...] = tok[scal[2]]
    columns = wg.shape[1]
    for i in range(4):
        total = jnp.sum(ssq[i], axis=1, keepdims=True)
        inverse = lax.rsqrt(total / wg.shape[0] + NORM_EPS)
        keep = inverse > 0.0
        gate = jnp.where(keep, acc[i, :, 0:columns] * inverse, 0.0)
        up = jnp.where(keep, acc[i, :, columns:] * inverse, 0.0)
        hidden[i] = (gate * sigmoid(gate) * up).astype(BF)


def gate_up(blocks, last, scal, own, other, wg, wu, *sofar):
    half = own[0].shape[2] - 16
    shapes = [(4, half, 2 * wg.shape[1]), (4, half, 128), (2, 16, 128)]
    if last:
        out_shape = [
            jax.ShapeDtypeStruct((4, half, wg.shape[1]), BF),
            jax.ShapeDtypeStruct((16, 128), F32),
        ]
        scratch = [pltpu.VMEM(shape, F32) for shape in shapes]
    else:
        out_shape, scratch = [jax.ShapeDtypeStruct(shape, F32) for shape in shapes], []
    values = (*own, *other, wg, wu, *sofar)
    return pl.pallas_call(
        functools.partial(gate_up_kernel, blocks, len(own), bool(sofar), last),
        out_shape=out_shape,
        in_specs=[IN_SMEM] + [IN_VMEM] * len(values),
        out_specs=[IN_VMEM] * len(out_shape),
        scratch_shapes=scratch,
        compiler_params=params(28),
        name=f"gate_up_{len(blocks)}",
    )(scal, *values)


def down_kernel(far, steps, scal, hidden, wd, out):
    core = lax.bitwise_and(scal[0], 1)
    if far:
        core = 1 - core
    width = out.shape[3]
    for i, second in enumerate(steps):
        for first in range(4):
            dx = first + core * (second - first)
            dy = second + core * (first - second)
            pipe, pair = plane_target(scal, dy, dx)
            cols = pl.ds(pl.multiple_of(pair * 2 * width, 128), 2 * width)
            product = jnp.dot(hidden[pipe * 2 + core], wd[:, cols], preferred_element_type=F32)
            out[4 * i + first, 0] = product[:, 0:width].astype(BF)
            out[4 * i + first, 1] = product[:, width:].astype(BF)


def down(far, steps, scal, hidden, wd):
    shape = (4 * len(steps), 2, hidden.shape[1], wd.shape[1] // N_TENSOR)
    return pl.pallas_call(
        functools.partial(down_kernel, far, steps),
        out_shape=jax.ShapeDtypeStruct(shape, BF),
        in_specs=[IN_SMEM] + [IN_VMEM] * 2,
        out_specs=IN_VMEM,
        compiler_params=params(20),
        name=f"down_{'far' if far else 'near'}_{len(steps)}",
    )(scal, hidden, wd)


def add(base, *parts):
    total = base.astype(F32)
    for part in parts:
        total = total + part.astype(F32)
    return total.astype(BF)


def expert_layer(scal, extra, arrived, wg, wu, wd):
    together = lax.optimization_barrier
    half, width = arrived.shape[0] // 2, arrived.shape[1]
    block = (half + 16, width)
    keep, send = small_call(halves_kernel, [block] * 2, scal, arrived, extra)
    (both,) = small_call(pair_kernel, [(2,) + block], scal, keep, from_flip(send, 1))
    lines = [both] + [from_axis(both, True, d) for d in (1, 2, 3)]
    low0, high0 = small_call(stack_kernel, [(2, 2) + block] * 2, None, *lines)
    low1, high3 = from_axis(low0, False, 1), from_axis(high0, False, 3)
    own = (low0, high0)
    blocks = {(0, 0): (0, 0), (0, 1): (1, 0)}
    sofar = gate_up(blocks, False, scal, own, [from_flip(v, 1) for v in own], wg, wu)
    low0, high0, low1, high3, sofar = together((low0, high0, low1, high3, sofar))
    up, dn = small_call(join_kernel, [(4, 2) + block] * 2, None, low1, high0, low0, high3)
    up, dn = from_axis(up, False, 1), from_axis(dn, False, 3)
    own = (low1, high3)
    blocks = {(1, 0): (0, 0), (3, 1): (1, 0)}
    sofar = gate_up(blocks, False, scal, own, [from_flip(v, 1) for v in own], wg, wu, *sofar)
    up, dn, sofar = together((up, dn, sofar))
    own = (up, dn)
    blocks = {(2, 0): (0, 0), (1, 1): (0, 2), (3, 0): (1, 0), (2, 1): (1, 2)}
    hidden, sums = gate_up(
        blocks, True, scal, own, [from_flip(v, 1) for v in own], wg, wu, *sofar
    )

    far = down(True, (2,), scal, hidden, wd)
    hidden, far = together((hidden, far))
    got = from_flip(far, 1)
    own = down(False, (2,), scal, hidden, wd)
    low2, high2 = add(own[:2], got[:2]), add(own[2:], got[2:])
    hidden, low2, high2 = together((hidden, low2, high2))
    low2, high2 = from_axis(low2, False, 3), from_axis(high2, False, 1)
    far = down(True, (0, 1, 3), scal, hidden, wd)
    hidden, far = together((hidden, far))
    got = from_flip(far, 1)
    own = down(False, (0, 1, 3), scal, hidden, wd)
    low1, high1, low3, high3 = ((own[i : i + 2], got[i : i + 2]) for i in range(4, 12, 2))
    up = jnp.concatenate([add(*low1, low2), add(*high1)])
    dn = jnp.concatenate([add(*low3), add(*high3, high2)])
    up, dn = together((from_axis(up, False, 3), from_axis(dn, False, 1)))
    line = add(own[:4], got[:4], up, dn)
    done = add(line[0], *(from_axis(line[d], True, 4 - d) for d in (1, 2, 3)))
    core = lax.bitwise_and(scal[0], 1)
    mine = lax.dynamic_index_in_dim(done, core, 0, keepdims=False)
    other = from_flip(lax.dynamic_index_in_dim(done, 1 - core, 0, keepdims=False), 1)
    first = core == 0
    rows = [jnp.where(first, mine, other), jnp.where(first, other, mine)]
    return jnp.concatenate(rows), sums


CORE_GROUPS = [list(range(0, 16, 2)), list(range(1, 16, 2))]


def exchange(value):
    return lax.all_to_all(
        value, "tensor", split_axis=0, concat_axis=0, axis_index_groups=CORE_GROUPS
    )


def product_blocks(scal, core, xt, wbuf):
    rows = xt.shape[1]
    for group in range(2):
        slots = []
        for j in range(group * 4, group * 4 + 4):
            t = j * 2 + core
            dp = lax.bitwise_xor(lax.shift_right_logical(t, 3), scal[2])
            dz = lax.bitwise_and(lax.bitwise_and(t, 7) - scal[3] + 8, 7)
            slots.append(dp * 8 + dz)
        left = jnp.concatenate([xt[slot] for slot in slots], axis=0)
        product = jnp.dot(left, wbuf[...], preferred_element_type=F32)
        for k, slot in enumerate(slots):
            yield group * 4 + k, slot, product[k * rows : (k + 1) * rows]


def store_block(out, j, product, squares):
    rows = product.shape[0]
    out[j, 0:rows] = product.astype(BF)
    high = squares.astype(BF)
    rest = squares - high.astype(F32)
    middle = rest.astype(BF)
    low = (rest - middle.astype(F32)).astype(BF)
    empty = jnp.zeros((16, product.shape[1] - 3 * rows), BF)
    wide = [jnp.broadcast_to(v.astype(F32), (16, rows)).astype(BF) for v in (high, middle, low)]
    out[j, rows : rows + 16] = jnp.concatenate(wide + [empty], axis=1)


def proj_far_kernel(scal, gain, *refs):
    n0, u1, d1, u2, d2, u3, d3, h4, l4, s1, s2, s3 = refs[:12]
    wq, wk, wv, out, xt, sq, wbuf = refs[12:]
    half = h4.shape[0]
    n4 = jnp.concatenate([h4[...], l4[...]], axis=0)
    pieces = {0: n0, 1: u1, 7: d1, 2: u2, 6: d2, 3: u3, 5: d3}
    pieces = {i: ref[...] for i, ref in pieces.items()}
    pieces.update({4: n4, 8: s1[0], 9: s1[1], 15: s1[2], 12: s3[...]})
    pieces.update({10: s2[0], 14: s2[1], 11: s2[2], 13: s2[3]})
    ones = jnp.ones((8, n0.shape[1]), BF)
    over_features = functools.partial(
        lax.dot_general,
        dimension_numbers=(((1,), (1,)), ((), ())),
        preferred_element_type=F32,
    )
    for i, value in pieces.items():
        rows = value.astype(F32)
        xt[i] = (rows * gain[...]).astype(BF)
        squares = rows * rows
        high = squares.astype(BF)
        low = (squares - high.astype(F32)).astype(BF)
        sq[i] = over_features(ones, high) + over_features(ones, low)
    qw = wq.shape[1]
    head = pl.ds(pl.multiple_of(scal[4] * HD, HD), HD)
    wbuf[:, 0:qw] = wq[...]
    wbuf[:, qw : qw + HD] = wk[:, head]
    wbuf[:, qw + HD :] = wv[:, head]
    core = 1 - lax.bitwise_and(scal[0], 1)
    for j, slot, product in product_blocks(scal, core, xt, wbuf):
        store_block(out, j, product, sq[slot][0:1])


def proj_near_kernel(scal, got, xt, sq, wbuf, out):
    rows = xt.shape[1]
    core = lax.bitwise_and(scal[0], 1)
    for j, slot, product in product_blocks(scal, core, xt, wbuf):
        parts = got[j, rows : rows + 16].astype(F32)
        squares = sq[slot][0:1]
        for k in (2, 1, 0):
            squares = squares + parts[0:1, k * rows : (k + 1) * rows]
        store_block(out, j, product + got[j, 0:rows].astype(F32), squares)


def projections(scal, gain, tokens, wq, wk, wv):
    rows, width = tokens[0].shape
    columns = wq.shape[1] + 2 * HD
    sums = jax.ShapeDtypeStruct((8, rows + 16, columns), BF)
    far, xt, sq, wbuf = pl.pallas_call(
        proj_far_kernel,
        out_shape=[
            sums,
            jax.ShapeDtypeStruct((16, rows, width), BF),
            jax.ShapeDtypeStruct((16, 8, rows), F32),
            jax.ShapeDtypeStruct((width, columns), BF),
        ],
        in_specs=[IN_SMEM] + [IN_VMEM] * 16,
        out_specs=[IN_VMEM] * 4,
        compiler_params=params(20),
        name="proj_far",
    )(scal, gain, *tokens, wq, wk, wv)
    got = from_flip(far, 1)
    near = pl.pallas_call(
        proj_near_kernel,
        out_shape=sums,
        in_specs=[IN_SMEM] + [IN_VMEM] * 4,
        out_specs=IN_VMEM,
        compiler_params=params(20),
        name="proj_near",
    )(scal, got, xt, sq, wbuf)
    total = jnp.sum(exchange(near).astype(F32), axis=0)
    parts = total[rows, : 3 * rows].reshape(3, rows)
    return total[:rows], parts[0] + (parts[1] + parts[2])


def attend_kernel(scal, q, kv0, kv1, out):
    rows = q.shape[0]
    heads = q.shape[1] // HD
    own = scal[0]
    core = lax.bitwise_and(own, 1)
    keys, values, places = [], [], []
    for dc, kv in enumerate((kv0, kv1)):
        for j in range(8):
            block = kv[j]
            keys.append(block[:, :HD])
            values.append(block[:, HD:])
            base = (2 * j + lax.bitwise_xor(core, dc)) * rows
            places.append(lax.broadcasted_iota(jnp.int32, (rows, rows), 1) + base)
    keys = jnp.concatenate(keys, axis=0)
    values = jnp.concatenate(values, axis=0)
    places = jnp.concatenate(places, axis=1)
    mine = lax.broadcasted_iota(jnp.int32, places.shape, 0) + own * rows
    allowed = places <= mine
    for h in range(heads):
        scores = lax.dot_general(
            q[:, h * HD : (h + 1) * HD],
            keys,
            (((1,), (1,)), ((), ())),
            preferred_element_type=F32,
        ) * (1.0 / math.sqrt(HD))
        scores = jnp.where(allowed, scores, -1e30)
        best = jnp.max(scores, axis=1, keepdims=True)
        weights = jnp.where(allowed, jnp.exp(scores - best), 0.0)
        total = jnp.sum(weights, axis=1, keepdims=True)
        mixed = jnp.dot(weights.astype(BF), values, preferred_element_type=F32)
        out[:, h * HD : (h + 1) * HD] = (mixed / total).astype(BF)


def attend(scal, q, kv0, kv1):
    return pl.pallas_call(
        attend_kernel,
        out_shape=jax.ShapeDtypeStruct(q.shape, BF),
        in_specs=[IN_SMEM] + [IN_VMEM] * 3,
        out_specs=IN_VMEM,
        compiler_params=params(24),
        name="attend",
    )(scal, q, kv0, kv1)


def gather_tokens(own):
    half = own.shape[0] // 2
    u1, d1 = from_z(own, 1), from_z(own, 7)
    s1 = from_pipe(jnp.stack([own, u1, d1]))
    u2, d2 = from_z(u1, 1), from_z(d1, 7)
    u3, d3 = from_z(u2, 1), from_z(d2, 7)
    u3, d3, s1 = lax.optimization_barrier((u3, d3, s1))
    s2 = from_pipe(jnp.stack([u2, d2, u3, d3]))
    h4, l4 = from_z(u3[:half], 1), from_z(d3[half:], 7)
    s3 = from_pipe(jnp.concatenate([h4, l4]))
    return (own, u1, d1, u2, d2, u3, d3, h4, l4, s1, s2, s3)


def on_device(
    stream,
    norm_gain,
    attn_gain,
    router,
    expert_ids,
    expert_slots,
    w_gate,
    w_up,
    w_down,
    w_query,
    w_key,
    w_value,
):
    token_rows, width = stream.shape
    features = width * N_TENSOR
    experts = router.shape[1]
    query_width = w_query.shape[1]
    heads_here = query_width // HD
    t = lax.axis_index("tensor")
    pipe = lax.axis_index("pipe")
    z = lax.axis_index("expert")
    kv_head = (pipe * 8 + z) * heads_here // (QH // KVH)
    yy = pipe * 2 + (t // 2) % 2
    scal = jnp.stack([t, yy, pipe, z, kv_head]).astype(jnp.int32)

    outgoing, extra = prepare(
        stream, norm_gain.reshape(1, width), router.T, expert_ids.T, expert_slots.T
    )
    scal, outgoing, extra = lax.optimization_barrier((scal, outgoing, extra))
    arrived = lax.all_to_all(outgoing, "expert", split_axis=0, concat_axis=0, tiled=True)
    expert_out, sums = expert_layer(scal, extra, arrived, w_gate[0], w_up[0], w_down[0])
    returned = lax.all_to_all(
        expert_out.reshape(experts, CAP, width),
        "expert",
        split_axis=0,
        concat_axis=0,
        axis_index_groups=[list(range(experts))[::-1]],
    ).reshape(experts * CAP, width)

    inverse = lax.rsqrt(sums[3] / features + NORM_EPS)
    first_share = jax.nn.sigmoid(inverse * sums[4])
    second_share = 1.0 - first_share

    slot_total = experts * CAP
    place = (experts - 1 - expert_ids) * CAP + expert_slots
    target = jnp.where(expert_slots >= 0, place, slot_total)
    slots = jnp.arange(slot_total, dtype=jnp.int32)
    stream_f = stream.astype(F32)
    wanted = jnp.concatenate([target[:, 0], target[:, 1]])
    picks = (wanted[:, None] == slots[None]).astype(BF)
    picked = jnp.dot(picks, returned, preferred_element_type=F32)
    moe_sum = (
        first_share[:, None] * picked[:token_rows] + second_share[:, None] * picked[token_rows:]
    )
    new_stream = (stream_f + moe_sum).astype(BF)

    tokens = gather_tokens(new_stream)
    own_proj, squares_two = projections(
        scal, attn_gain.reshape(1, width), tokens, w_query, w_key, w_value
    )
    inverse_two = lax.rsqrt(squares_two / features + NORM_EPS)[:, None]
    own_proj = jnp.where(inverse_two > 0.0, own_proj * inverse_two, 0.0).astype(BF)
    queries = own_proj[:, :query_width]
    kv = own_proj[:, query_width:]
    kv = exchange(jnp.broadcast_to(kv[None], (8,) + kv.shape))
    attended = attend(scal, queries, kv, from_flip(kv, 1))
    return (new_stream, attended)


def solution(mesh):
    in_specs = (
        P(("pipe", "expert"), "tensor"),
        P("tensor"),
        P("tensor"),
        P("tensor", None),
        P(("pipe", "expert"), None),
        P(("pipe", "expert"), None),
        P("expert", None, ("pipe", "tensor")),
        P("expert", None, ("pipe", "tensor")),
        P("expert", ("pipe", "tensor"), None),
        P("tensor", ("pipe", "expert")),
        P("tensor", None),
        P("tensor", None),
    )
    out_specs = (P(("pipe", "expert"), "tensor"), P("tensor", ("pipe", "expert")))
    return jax.shard_map(
        on_device, mesh=mesh, in_specs=in_specs, out_specs=out_specs, check_vma=False
    )
```

```python
import functools
import math

import jax
import jax.numpy as jnp
from jax import lax
from jax.experimental import pallas as pl
from jax.experimental.pallas import tpu as pltpu
from jax.sharding import PartitionSpec as P

HD = 128
QH = 48
KVH = 8
CAP = 40
NORM_EPS = 1e-05
N_TENSOR = 16
BF = jnp.bfloat16
F32 = jnp.float32


def from_axis(value, first, d):
    pairs = []
    for x in range(4):
        for yy in range(4):
            for core in range(2):
                along_x = (core == 0) == first
                tx = (x - d) % 4 if along_x else x
                ty = yy if along_x else (yy - d) % 4
                source = (yy // 2) * 16 + x * 4 + (yy % 2) * 2 + core
                pairs.append((source, (ty // 2) * 16 + tx * 4 + (ty % 2) * 2 + core))
    return lax.ppermute(value, ("pipe", "tensor"), pairs)


def from_flip(value, bit):
    return lax.ppermute(value, "tensor", [(i, i ^ bit) for i in range(16)])


def from_z(value, dz):
    return lax.ppermute(value, "expert", [(i, (i - dz) % 8) for i in range(8)])


def from_pipe(value):
    return lax.ppermute(value, "pipe", [(0, 1), (1, 0)])


def plane_target(scal, dy, dx):
    tx = lax.bitwise_and(lax.shift_right_logical(scal[0], 2) + dx, 3)
    ty = lax.bitwise_and(scal[1] + dy, 3)
    return lax.shift_right_logical(ty, 1), tx * 2 + lax.bitwise_and(ty, 1)


def sigmoid(v):
    return 1.0 / (1.0 + jnp.exp(-v))


IN_VMEM = pl.BlockSpec(memory_space=pltpu.VMEM)
IN_SMEM = pl.BlockSpec(memory_space=pltpu.SMEM)


def params(mib):
    return pltpu.CompilerParams(vmem_limit_bytes=mib * 1024 * 1024)


def prepare_kernel(stream, gain, router, ids, slots, outgoing, extra):
    experts = router.shape[0]
    tokens, width = stream.shape
    wanted = jnp.where(slots[...] >= 0, ids[...] * CAP + slots[...], experts * CAP)
    slot = lax.broadcasted_iota(jnp.int32, (experts * CAP, tokens), 0)
    chosen = (slot == wanted[0:1]) | (slot == wanted[1:2])
    chosen = jnp.where(chosen, 1.0, 0.0).astype(BF)
    rows = stream[...]
    outgoing[...] = jnp.dot(chosen, rows, preferred_element_type=F32).astype(BF)
    rows = rows.astype(F32)
    over_features = functools.partial(
        lax.dot_general,
        dimension_numbers=(((1,), (1,)), ((), ())),
        preferred_element_type=F32,
    )
    squares = rows * rows
    high = squares.astype(BF)
    low = (squares - high.astype(F32)).astype(BF)
    ones = jnp.ones((8, width), BF)
    square_sums = (over_features(ones, high) + over_features(ones, low))[0:1]
    logits = over_features(router[...], rows * gain[...], precision=lax.Precision.HIGHEST)
    number = lax.broadcasted_iota(jnp.int32, (experts, tokens), 0)
    apart = jnp.sum(jnp.where(number == ids[0:1], logits, 0.0), axis=0, keepdims=True) - jnp.sum(
        jnp.where(number == ids[1:2], logits, 0.0), axis=0, keepdims=True
    )

    def split(value):
        first = value.astype(BF).astype(F32)
        rest = value - first
        second = rest.astype(BF).astype(F32)
        return first, second, (rest - second).astype(BF).astype(F32)

    lines = list(split(gain[...]))
    empty = [jnp.zeros((1, width - 3 * tokens), F32)] if width > 3 * tokens else []
    lines += [jnp.concatenate(list(split(v)) + empty, axis=1) for v in (square_sums, apart)]
    line = lax.broadcasted_iota(jnp.int32, (16, width), 0)
    out = jnp.zeros((16, width), F32)
    for i, value in enumerate(lines):
        out = jnp.where(line == i, value, out)
    extra[...] = out.astype(BF)


def prepare(stream, gain, router, ids, slots):
    experts = router.shape[0]
    width = stream.shape[1]
    return pl.pallas_call(
        prepare_kernel,
        out_shape=[
            jax.ShapeDtypeStruct((experts * CAP, width), BF),
            jax.ShapeDtypeStruct((16, width), BF),
        ],
        in_specs=[IN_VMEM] * 5,
        out_specs=[IN_VMEM] * 2,
        compiler_params=params(8),
        name="prepare",
    )(stream, gain, router, ids, slots)


def halves_kernel(scal, arrived, extra, keep, send):
    core = lax.bitwise_and(scal[0], 1)
    half = arrived.shape[0] // 2
    blocks = arrived.shape[0] // CAP
    rows = arrived[...].astype(F32)
    rows = [rows[j * CAP : (j + 1) * CAP] for j in reversed(range(blocks))]
    first = jnp.concatenate(rows[: blocks // 2], axis=0).astype(BF)
    second = jnp.concatenate(rows[blocks // 2 :], axis=0).astype(BF)
    keep[0:half] = jnp.where(core == 0, first, second)
    send[0:half] = jnp.where(core == 0, second, first)
    keep[half : half + 16] = extra[...]
    send[half : half + 16] = extra[...]


def pair_kernel(scal, own, got, out):
    core = lax.bitwise_and(scal[0], 1)
    out[core] = own[...]
    out[1 - core] = got[...]


def stack_kernel(v0, v1, v2, v3, low, high):
    low[0] = v0[...]
    low[1] = v1[...]
    high[0] = v2[...]
    high[1] = v3[...]


def join_kernel(v0, v1, v2, v3, up, down):
    up[0:2] = v0[...]
    up[2:4] = v1[...]
    down[0:2] = v2[...]
    down[2:4] = v3[...]


def small_call(kernel, shapes, scal, *values):
    specs = [IN_VMEM] * len(values)
    if scal is not None:
        specs, values = [IN_SMEM] + specs, (scal,) + values
    return pl.pallas_call(
        kernel,
        out_shape=[jax.ShapeDtypeStruct(shape, BF) for shape in shapes],
        in_specs=specs,
        out_specs=[IN_VMEM] * len(shapes),
        compiler_params=params(8),
        name=kernel.__name__,
    )(*values)


def accumulate(scal, piece, steps, wg, wu, acc, ssq):
    columns = wg.shape[1]
    half = acc.shape[1]
    for (parity, dx), segments in steps.items():
        _, pair = plane_target(scal, parity, dx)
        scaled = []
        squares = 0.0
        for core in range(2):
            blocks = [piece(kind, dy, dx) for kind, dy in segments]
            blocks = [ref.at[index, core] for ref, index in blocks]
            parts = blocks[0][half : half + 16].astype(F32)
            gain = parts[0:1] + parts[1:2] + parts[2:3]
            rows = jnp.concatenate([block[0:half] for block in blocks], axis=0).astype(F32)
            width = rows.shape[1]
            scaled.append((rows * gain).astype(BF))
            rows = rows * rows
            for j in range(width // 128):
                squares = squares + rows[:, j * 128 : (j + 1) * 128]
        left = jnp.concatenate(scaled, axis=1)
        rows = pl.ds(pl.multiple_of(pair * 2 * width, 128), 2 * width)
        gate = jnp.dot(left, wg[rows, :], preferred_element_type=F32)
        up = jnp.dot(left, wu[rows, :], preferred_element_type=F32)
        for k, (kind, dy) in enumerate(segments):
            pipe, _ = plane_target(scal, dy, dx)
            to = pipe * 2 + (kind == "b")
            here = slice(k * half, (k + 1) * half)
            acc[to, :, 0:columns] += gate[here]
            acc[to, :, columns:] += up[here]
            ssq[to] += squares[here]


def steps_of(blocks, kinds):
    steps = {}
    for parity in range(2):
        for dx in range(4):
            segments = []
            for dy in (parity, parity + 2):
                segments += [("a", dy)] if "a" in kinds and (dy, dx // 2) in blocks else []
                segments += [("b", dy)] if "b" in kinds and (dx, dy // 2) in blocks else []
            if segments:
                steps[(parity, dx)] = segments
    return steps


def on_each_core(scal, own, other, body):
    core = lax.bitwise_and(scal[0], 1)
    pl.when(core == 0)(lambda: body(own or None, other or None))
    pl.when(core == 1)(lambda: body(other or None, own or None))


def gate_up_kernel(blocks, counts, started, last, scal, *refs):
    own, refs = refs[: counts[0]], refs[counts[0] :]
    other, refs = refs[: counts[1]], refs[counts[1] :]
    (wg, wu), refs = refs[:2], refs[2:]
    acc, ssq, tok = refs[-3:]
    half = acc.shape[1]
    if started:
        for ref, before in zip((acc, ssq, tok), refs):
            ref[...] = before[...]
    else:
        for ref in (acc, ssq, tok):
            ref[...] = jnp.zeros_like(ref)

    def body(half_a, half_b):
        def piece(kind, dy, dx):
            first, second, table = (dx, dy, half_a) if kind == "a" else (dy, dx, half_b)
            array, start = blocks[(second, first // 2)]
            return table[array], start + first % 2

        kinds = ("a" if half_a else "") + ("b" if half_b else "")
        accumulate(scal, piece, steps_of(blocks, kinds), wg, wu, acc, ssq)
        if not half_a:
            return
        for (dy, _), (array, start) in blocks.items():
            pipe, _ = plane_target(scal, dy, 0)
            for at in (start, start + 1):
                for core in range(2):
                    parts = half_a[array][at, core, half : half + 16].astype(F32)
                    tok[pipe] += parts[:, 0:128] + parts[:, 128:256] + parts[:, 256:384]

    on_each_core(scal, own, other, body)
    if not last:
        return
    hidden, sums = refs[3:5]
    sums[...] = tok[scal[2]]
    columns = wg.shape[1]
    for i in range(4):
        total = jnp.sum(ssq[i], axis=1, keepdims=True)
        inverse = lax.rsqrt(total / wg.shape[0] + NORM_EPS)
        keep = inverse > 0.0
        gate = jnp.where(keep, acc[i, :, 0:columns] * inverse, 0.0)
        up = jnp.where(keep, acc[i, :, columns:] * inverse, 0.0)
        hidden[i] = (gate * sigmoid(gate) * up).astype(BF)


def gate_up(blocks, last, scal, own, other, wg, wu, *sofar):
    half = (*own, *other)[0].shape[2] - 16
    shapes = [(4, half, 2 * wg.shape[1]), (4, half, 128), (2, 16, 128)]
    if last:
        out_shape = [
            jax.ShapeDtypeStruct((4, half, wg.shape[1]), BF),
            jax.ShapeDtypeStruct((16, 128), F32),
        ]
        scratch = [pltpu.VMEM(shape, F32) for shape in shapes]
    else:
        out_shape, scratch = [jax.ShapeDtypeStruct(shape, F32) for shape in shapes], []
    values = (*own, *other, wg, wu, *sofar)
    return pl.pallas_call(
        functools.partial(
            gate_up_kernel, blocks, (len(own), len(other)), bool(sofar), last
        ),
        out_shape=out_shape,
        in_specs=[IN_SMEM] + [IN_VMEM] * len(values),
        out_specs=[IN_VMEM] * len(out_shape),
        scratch_shapes=scratch,
        compiler_params=params(28),
        name=f"gate_up_{len(blocks)}_{len(own)}_{len(other)}",
    )(scal, *values)


def down_kernel(far, steps, scal, hidden, wd, out):
    core = lax.bitwise_and(scal[0], 1)
    if far:
        core = 1 - core
    width = out.shape[3]
    for i, second in enumerate(steps):
        for first in range(4):
            dx = first + core * (second - first)
            dy = second + core * (first - second)
            pipe, pair = plane_target(scal, dy, dx)
            cols = pl.ds(pl.multiple_of(pair * 2 * width, 128), 2 * width)
            product = jnp.dot(hidden[pipe * 2 + core], wd[:, cols], preferred_element_type=F32)
            out[4 * i + first, 0] = product[:, 0:width].astype(BF)
            out[4 * i + first, 1] = product[:, width:].astype(BF)


def down(far, steps, scal, hidden, wd):
    shape = (4 * len(steps), 2, hidden.shape[1], wd.shape[1] // N_TENSOR)
    return pl.pallas_call(
        functools.partial(down_kernel, far, steps),
        out_shape=jax.ShapeDtypeStruct(shape, BF),
        in_specs=[IN_SMEM] + [IN_VMEM] * 2,
        out_specs=IN_VMEM,
        compiler_params=params(20),
        name=f"down_{'far' if far else 'near'}_{len(steps)}",
    )(scal, hidden, wd)


def add(base, *parts):
    total = base.astype(F32)
    for part in parts:
        total = total + part.astype(F32)
    return total.astype(BF)


def expert_layer(scal, extra, arrived, wg, wu, wd):
    together = lax.optimization_barrier
    half, width = arrived.shape[0] // 2, arrived.shape[1]
    block = (half + 16, width)
    keep, send = small_call(halves_kernel, [block] * 2, scal, arrived, extra)
    (both,) = small_call(pair_kernel, [(2,) + block], scal, keep, from_flip(send, 1))
    lines = [both] + [from_axis(both, True, d) for d in (1, 2, 3)]
    low0, high0 = small_call(stack_kernel, [(2, 2) + block] * 2, None, *lines)
    low1, high3 = from_axis(low0, False, 1), from_axis(high0, False, 3)
    own = (low0, high0)
    blocks = {(0, 0): (0, 0), (0, 1): (1, 0)}
    sofar = gate_up(blocks, False, scal, own, [from_flip(v, 1) for v in own], wg, wu)
    low0, high0, low1, high3, sofar = together((low0, high0, low1, high3, sofar))
    up, dn = small_call(join_kernel, [(4, 2) + block] * 2, None, low1, high0, low0, high3)
    up, dn = from_axis(up, False, 1), from_axis(dn, False, 3)
    own = (low1, high3)
    blocks = {(1, 0): (0, 0), (3, 1): (1, 0)}
    sofar = gate_up(blocks, False, scal, own, [from_flip(v, 1) for v in own], wg, wu, *sofar)
    up, dn, sofar = together((up, dn, sofar))
    own = (up, dn)
    blocks = {(2, 0): (0, 0), (1, 1): (0, 2), (3, 0): (1, 0), (2, 1): (1, 2)}
    sofar = gate_up(blocks, False, scal, own, (), wg, wu, *sofar)
    other = [from_flip(v, 1) for v in own]
    hidden, sums = gate_up(blocks, True, scal, (), other, wg, wu, *sofar)

    far = down(True, (2,), scal, hidden, wd)
    hidden, far = together((hidden, far))
    got = from_flip(far, 1)
    own = down(False, (2,), scal, hidden, wd)
    far = down(True, (0, 1, 3), scal, hidden, wd)
    low2, high2 = add(own[:2], got[:2]), add(own[2:], got[2:])
    hidden, low2, high2, far = together((hidden, low2, high2, far))
    low2, high2 = from_axis(low2, False, 3), from_axis(high2, False, 1)
    got = from_flip(far, 1)
    own = down(False, (0, 1, 3), scal, hidden, wd)
    low1, high1, low3, high3 = ((own[i : i + 2], got[i : i + 2]) for i in range(4, 12, 2))
    up = jnp.concatenate([add(*low1, low2), add(*high1)])
    dn = jnp.concatenate([add(*low3), add(*high3, high2)])
    up, dn = together((from_axis(up, False, 3), from_axis(dn, False, 1)))
    line = add(own[:4], got[:4], up, dn)
    done = add(line[0], *(from_axis(line[d], True, 4 - d) for d in (1, 2, 3)))
    core = lax.bitwise_and(scal[0], 1)
    mine = lax.dynamic_index_in_dim(done, core, 0, keepdims=False)
    other = from_flip(lax.dynamic_index_in_dim(done, 1 - core, 0, keepdims=False), 1)
    first = core == 0
    rows = [jnp.where(first, mine, other), jnp.where(first, other, mine)]
    return jnp.concatenate(rows), sums


CORE_GROUPS = [list(range(0, 16, 2)), list(range(1, 16, 2))]


def exchange(value):
    return lax.all_to_all(
        value, "tensor", split_axis=0, concat_axis=0, axis_index_groups=CORE_GROUPS
    )


def from_all(value):
    groups = [group[::-1] for group in CORE_GROUPS]
    value = jnp.broadcast_to(value[None], (8,) + value.shape)
    return lax.all_to_all(
        value, "tensor", split_axis=0, concat_axis=0, axis_index_groups=groups
    )


def product_blocks(scal, core, xt, wbuf):
    rows = xt.shape[1]
    for group in range(2):
        slots = []
        for j in range(group * 4, group * 4 + 4):
            t = j * 2 + core
            dp = lax.bitwise_xor(lax.shift_right_logical(t, 3), scal[2])
            dz = lax.bitwise_and(lax.bitwise_and(t, 7) - scal[3] + 8, 7)
            slots.append(dp * 8 + dz)
        left = jnp.concatenate([xt[slot] for slot in slots], axis=0)
        product = jnp.dot(left, wbuf[...], preferred_element_type=F32)
        for k, slot in enumerate(slots):
            yield group * 4 + k, slot, product[k * rows : (k + 1) * rows]


def store_block(out, j, product, squares):
    rows = product.shape[0]
    out[j, 0:rows] = product.astype(BF)
    high = squares.astype(BF)
    rest = squares - high.astype(F32)
    middle = rest.astype(BF)
    low = (rest - middle.astype(F32)).astype(BF)
    empty = jnp.zeros((16, product.shape[1] - 3 * rows), BF)
    wide = [jnp.broadcast_to(v.astype(F32), (16, rows)).astype(BF) for v in (high, middle, low)]
    out[j, rows : rows + 16] = jnp.concatenate(wide + [empty], axis=1)


def proj_far_kernel(scal, gain, *refs):
    n0, u1, d1, u2, d2, u3, d3, h4, l4, s1, s2, s3 = refs[:12]
    wq, wk, wv, out, xt, sq, wbuf = refs[12:]
    half = h4.shape[0]
    n4 = jnp.concatenate([h4[...], l4[...]], axis=0)
    pieces = {0: n0, 1: u1, 7: d1, 2: u2, 6: d2, 3: u3, 5: d3}
    pieces = {i: ref[...] for i, ref in pieces.items()}
    pieces.update({4: n4, 8: s1[0], 9: s1[1], 15: s1[2], 12: s3[...]})
    pieces.update({10: s2[0], 14: s2[1], 11: s2[2], 13: s2[3]})
    ones = jnp.ones((8, n0.shape[1]), BF)
    over_features = functools.partial(
        lax.dot_general,
        dimension_numbers=(((1,), (1,)), ((), ())),
        preferred_element_type=F32,
    )
    for i, value in pieces.items():
        rows = value.astype(F32)
        xt[i] = (rows * gain[...]).astype(BF)
        squares = rows * rows
        high = squares.astype(BF)
        low = (squares - high.astype(F32)).astype(BF)
        sq[i] = over_features(ones, high) + over_features(ones, low)
    qw = wq.shape[1]
    head = pl.ds(pl.multiple_of(scal[4] * HD, HD), HD)
    wbuf[:, 0:qw] = wq[...]
    wbuf[:, qw : qw + HD] = wk[:, head]
    wbuf[:, qw + HD :] = wv[:, head]
    core = 1 - lax.bitwise_and(scal[0], 1)
    for j, slot, product in product_blocks(scal, core, xt, wbuf):
        store_block(out, j, product, sq[slot][0:1])


def proj_near_kernel(scal, got, xt, sq, wbuf, out):
    rows = xt.shape[1]
    core = lax.bitwise_and(scal[0], 1)
    for j, slot, product in product_blocks(scal, core, xt, wbuf):
        parts = got[j, rows : rows + 16].astype(F32)
        squares = sq[slot][0:1]
        for k in (2, 1, 0):
            squares = squares + parts[0:1, k * rows : (k + 1) * rows]
        store_block(out, j, product + got[j, 0:rows].astype(F32), squares)


def projections(scal, gain, tokens, wq, wk, wv):
    rows, width = tokens[0].shape
    columns = wq.shape[1] + 2 * HD
    sums = jax.ShapeDtypeStruct((8, rows + 16, columns), BF)
    far, xt, sq, wbuf = pl.pallas_call(
        proj_far_kernel,
        out_shape=[
            sums,
            jax.ShapeDtypeStruct((16, rows, width), BF),
            jax.ShapeDtypeStruct((16, 8, rows), F32),
            jax.ShapeDtypeStruct((width, columns), BF),
        ],
        in_specs=[IN_SMEM] + [IN_VMEM] * 16,
        out_specs=[IN_VMEM] * 4,
        compiler_params=params(20),
        name="proj_far",
    )(scal, gain, *tokens, wq, wk, wv)
    got = from_flip(far, 1)
    near = pl.pallas_call(
        proj_near_kernel,
        out_shape=sums,
        in_specs=[IN_SMEM] + [IN_VMEM] * 4,
        out_specs=IN_VMEM,
        compiler_params=params(20),
        name="proj_near",
    )(scal, got, xt, sq, wbuf)
    total = jnp.sum(exchange(near).astype(F32), axis=0)
    parts = total[rows, : 3 * rows].reshape(3, rows)
    return total[:rows], parts[0] + (parts[1] + parts[2])


def attend_kernel(far, scal, q, kv, *refs):
    rows = q.shape[0]
    heads = q.shape[1] // HD
    own = scal[0]
    core = lax.bitwise_and(own, 1)
    core = 1 - core if far else core
    keys, values, places = [], [], []
    for j in range(8):
        block = kv[j]
        keys.append(block[:, :HD])
        values.append(block[:, HD:])
        base = (14 - 2 * j + core) * rows
        places.append(lax.broadcasted_iota(jnp.int32, (rows, rows), 1) + base)
    keys = jnp.concatenate(keys, axis=0)
    values = jnp.concatenate(values, axis=0)
    places = jnp.concatenate(places, axis=1)
    mine = lax.broadcasted_iota(jnp.int32, places.shape, 0) + own * rows
    allowed = places <= mine
    for h in range(heads):
        here = slice(h * HD, (h + 1) * HD)
        scores = lax.dot_general(
            q[:, here], keys, (((1,), (1,)), ((), ())), preferred_element_type=F32
        ) * (1.0 / math.sqrt(HD))
        scores = jnp.where(allowed, scores, -1e30)
        best = jnp.max(scores, axis=1, keepdims=True)
        if far:
            before, bests, totals, out = refs
            old = bests[:, here][:, 0:1]
            best = jnp.maximum(best, old)
        weights = jnp.where(allowed, jnp.exp(scores - best), 0.0)
        total = jnp.sum(weights, axis=1, keepdims=True)
        mixed = jnp.dot(weights.astype(BF), values, preferred_element_type=F32)
        if far:
            shrink = jnp.exp(old - best)
            total = total + totals[:, here][:, 0:1] * shrink
            out[:, here] = ((mixed + before[:, here] * shrink) / total).astype(BF)
        else:
            mixed_out, bests, totals = refs
            mixed_out[:, here] = mixed
            bests[:, here] = jnp.broadcast_to(best, mixed.shape)
            totals[:, here] = jnp.broadcast_to(total, mixed.shape)


def attend(far, scal, q, kv, *sofar):
    shapes = [jax.ShapeDtypeStruct(q.shape, BF)] if far else [jax.ShapeDtypeStruct(q.shape, F32)] * 3
    return pl.pallas_call(
        functools.partial(attend_kernel, far),
        out_shape=shapes,
        in_specs=[IN_SMEM] + [IN_VMEM] * (2 + len(sofar)),
        out_specs=[IN_VMEM] * len(shapes),
        compiler_params=params(24),
        name="attend_far" if far else "attend_near",
    )(scal, q, kv, *sofar)


def gather_tokens(own):
    half = own.shape[0] // 2
    u1, d1 = from_z(own, 1), from_z(own, 7)
    s1 = from_pipe(jnp.stack([own, u1, d1]))
    u2, d2 = from_z(u1, 1), from_z(d1, 7)
    u3, d3 = from_z(u2, 1), from_z(d2, 7)
    u3, d3, s1 = lax.optimization_barrier((u3, d3, s1))
    s2 = from_pipe(jnp.stack([u2, d2, u3, d3]))
    h4, l4 = from_z(u3[:half], 1), from_z(d3[half:], 7)
    s3 = from_pipe(jnp.concatenate([h4, l4]))
    return (own, u1, d1, u2, d2, u3, d3, h4, l4, s1, s2, s3)


def on_device(
    stream,
    norm_gain,
    attn_gain,
    router,
    expert_ids,
    expert_slots,
    w_gate,
    w_up,
    w_down,
    w_query,
    w_key,
    w_value,
):
    token_rows, width = stream.shape
    features = width * N_TENSOR
    experts = router.shape[1]
    query_width = w_query.shape[1]
    heads_here = query_width // HD
    t = lax.axis_index("tensor")
    pipe = lax.axis_index("pipe")
    z = lax.axis_index("expert")
    kv_head = (pipe * 8 + z) * heads_here // (QH // KVH)
    yy = pipe * 2 + (t // 2) % 2
    scal = jnp.stack([t, yy, pipe, z, kv_head]).astype(jnp.int32)

    outgoing, extra = prepare(
        stream, norm_gain.reshape(1, width), router.T, expert_ids.T, expert_slots.T
    )
    scal, outgoing, extra = lax.optimization_barrier((scal, outgoing, extra))
    arrived = lax.all_to_all(outgoing, "expert", split_axis=0, concat_axis=0, tiled=True)
    expert_out, sums = expert_layer(scal, extra, arrived, w_gate[0], w_up[0], w_down[0])
    returned = lax.all_to_all(
        expert_out.reshape(experts, CAP, width),
        "expert",
        split_axis=0,
        concat_axis=0,
        axis_index_groups=[list(range(experts))[::-1]],
    ).reshape(experts * CAP, width)

    inverse = lax.rsqrt(sums[3] / features + NORM_EPS)
    first_share = jax.nn.sigmoid(inverse * sums[4])
    second_share = 1.0 - first_share

    slot_total = experts * CAP
    place = (experts - 1 - expert_ids) * CAP + expert_slots
    target = jnp.where(expert_slots >= 0, place, slot_total)
    slots = jnp.arange(slot_total, dtype=jnp.int32)
    stream_f = stream.astype(F32)
    wanted = jnp.concatenate([target[:, 0], target[:, 1]])
    picks = (wanted[:, None] == slots[None]).astype(BF)
    picked = jnp.dot(picks, returned, preferred_element_type=F32)
    moe_sum = (
        first_share[:, None] * picked[:token_rows] + second_share[:, None] * picked[token_rows:]
    )
    new_stream = (stream_f + moe_sum).astype(BF)

    tokens = gather_tokens(new_stream)
    own_proj, squares_two = projections(
        scal, attn_gain.reshape(1, width), tokens, w_query, w_key, w_value
    )
    inverse_two = lax.rsqrt(squares_two / features + NORM_EPS)[:, None]
    own_proj = jnp.where(inverse_two > 0.0, own_proj * inverse_two, 0.0).astype(BF)
    queries = own_proj[:, :query_width]
    kv = own_proj[:, query_width:]
    kv = from_all(kv)
    other = from_flip(kv, 1)
    (attended,) = attend(True, scal, queries, other, *attend(False, scal, queries, kv))
    return (new_stream, attended)


def solution(mesh):
    in_specs = (
        P(("pipe", "expert"), "tensor"),
        P("tensor"),
        P("tensor"),
        P("tensor", None),
        P(("pipe", "expert"), None),
        P(("pipe", "expert"), None),
        P("expert", None, ("pipe", "tensor")),
        P("expert", None, ("pipe", "tensor")),
        P("expert", ("pipe", "tensor"), None),
        P("tensor", ("pipe", "expert")),
        P("tensor", None),
        P("tensor", None),
    )
    out_specs = (P(("pipe", "expert"), "tensor"), P("tensor", ("pipe", "expert")))
    return jax.shard_map(
        on_device, mesh=mesh, in_specs=in_specs, out_specs=out_specs, check_vma=False
    )
```

```python
import functools
import math

import jax
import jax.numpy as jnp
from jax import lax
from jax.experimental import pallas as pl
from jax.experimental.pallas import tpu as pltpu
from jax.sharding import PartitionSpec as P

HD = 128
QH = 48
KVH = 8
CAP = 40
NORM_EPS = 1e-05
N_TENSOR = 16
BF = jnp.bfloat16
F32 = jnp.float32


def from_axis(value, first, d):
    pairs = []
    for x in range(4):
        for yy in range(4):
            for core in range(2):
                along_x = (core == 0) == first
                tx = (x - d) % 4 if along_x else x
                ty = yy if along_x else (yy - d) % 4
                source = (yy // 2) * 16 + x * 4 + (yy % 2) * 2 + core
                pairs.append((source, (ty // 2) * 16 + tx * 4 + (ty % 2) * 2 + core))
    return lax.ppermute(value, ("pipe", "tensor"), pairs)


def from_flip(value, bit):
    return lax.ppermute(value, "tensor", [(i, i ^ bit) for i in range(16)])


def from_z(value, dz):
    return lax.ppermute(value, "expert", [(i, (i - dz) % 8) for i in range(8)])


def from_pipe(value):
    return lax.ppermute(value, "pipe", [(0, 1), (1, 0)])


def plane_target(scal, dy, dx):
    tx = lax.bitwise_and(lax.shift_right_logical(scal[0], 2) + dx, 3)
    ty = lax.bitwise_and(scal[1] + dy, 3)
    return lax.shift_right_logical(ty, 1), tx * 2 + lax.bitwise_and(ty, 1)


def sigmoid(v):
    return 1.0 / (1.0 + jnp.exp(-v))


IN_VMEM = pl.BlockSpec(memory_space=pltpu.VMEM)
IN_SMEM = pl.BlockSpec(memory_space=pltpu.SMEM)


def params(mib):
    return pltpu.CompilerParams(vmem_limit_bytes=mib * 1024 * 1024)


def prepare_kernel(stream, gain, router, ids, slots, outgoing, extra):
    experts = router.shape[0]
    tokens, width = stream.shape
    wanted = jnp.where(slots[...] >= 0, ids[...] * CAP + slots[...], experts * CAP)
    slot = lax.broadcasted_iota(jnp.int32, (experts * CAP, tokens), 0)
    chosen = (slot == wanted[0:1]) | (slot == wanted[1:2])
    chosen = jnp.where(chosen, 1.0, 0.0).astype(BF)
    rows = stream[...]
    outgoing[...] = jnp.dot(chosen, rows, preferred_element_type=F32).astype(BF)
    rows = rows.astype(F32)
    over_features = functools.partial(
        lax.dot_general,
        dimension_numbers=(((1,), (1,)), ((), ())),
        preferred_element_type=F32,
    )
    squares = rows * rows
    high = squares.astype(BF)
    low = (squares - high.astype(F32)).astype(BF)
    ones = jnp.ones((8, width), BF)
    square_sums = (over_features(ones, high) + over_features(ones, low))[0:1]
    logits = over_features(router[...], rows * gain[...], precision=lax.Precision.HIGHEST)
    number = lax.broadcasted_iota(jnp.int32, (experts, tokens), 0)
    apart = jnp.sum(jnp.where(number == ids[0:1], logits, 0.0), axis=0, keepdims=True) - jnp.sum(
        jnp.where(number == ids[1:2], logits, 0.0), axis=0, keepdims=True
    )

    def split(value):
        first = value.astype(BF).astype(F32)
        rest = value - first
        second = rest.astype(BF).astype(F32)
        return first, second, (rest - second).astype(BF).astype(F32)

    lines = list(split(gain[...]))
    empty = [jnp.zeros((1, width - 3 * tokens), F32)] if width > 3 * tokens else []
    lines += [jnp.concatenate(list(split(v)) + empty, axis=1) for v in (square_sums, apart)]
    line = lax.broadcasted_iota(jnp.int32, (16, width), 0)
    out = jnp.zeros((16, width), F32)
    for i, value in enumerate(lines):
        out = jnp.where(line == i, value, out)
    extra[...] = out.astype(BF)


def prepare(stream, gain, router, ids, slots):
    experts = router.shape[0]
    width = stream.shape[1]
    return pl.pallas_call(
        prepare_kernel,
        out_shape=[
            jax.ShapeDtypeStruct((experts * CAP, width), BF),
            jax.ShapeDtypeStruct((16, width), BF),
        ],
        in_specs=[IN_VMEM] * 5,
        out_specs=[IN_VMEM] * 2,
        compiler_params=params(8),
        name="prepare",
    )(stream, gain, router, ids, slots)


def halves_kernel(scal, arrived, extra, keep, send):
    core = lax.bitwise_and(scal[0], 1)
    half = arrived.shape[0] // 2
    blocks = arrived.shape[0] // CAP
    rows = arrived[...].astype(F32)
    rows = [rows[j * CAP : (j + 1) * CAP] for j in reversed(range(blocks))]
    first = jnp.concatenate(rows[: blocks // 2], axis=0).astype(BF)
    second = jnp.concatenate(rows[blocks // 2 :], axis=0).astype(BF)
    keep[0:half] = jnp.where(core == 0, first, second)
    send[0:half] = jnp.where(core == 0, second, first)
    keep[half : half + 16] = extra[...]
    send[half : half + 16] = extra[...]


def pair_kernel(scal, own, got, out):
    core = lax.bitwise_and(scal[0], 1)
    out[core] = own[...]
    out[1 - core] = got[...]


def stack_kernel(v0, v1, v2, v3, low, high):
    low[0] = v0[...]
    low[1] = v1[...]
    high[0] = v2[...]
    high[1] = v3[...]


def join_kernel(v0, v1, v2, v3, up, down):
    up[0:2] = v0[...]
    up[2:4] = v1[...]
    down[0:2] = v2[...]
    down[2:4] = v3[...]


def small_call(kernel, shapes, scal, *values):
    specs = [IN_VMEM] * len(values)
    if scal is not None:
        specs, values = [IN_SMEM] + specs, (scal,) + values
    return pl.pallas_call(
        kernel,
        out_shape=[jax.ShapeDtypeStruct(shape, BF) for shape in shapes],
        in_specs=specs,
        out_specs=[IN_VMEM] * len(shapes),
        compiler_params=params(8),
        name=kernel.__name__,
    )(*values)


def accumulate(scal, piece, steps, wg, wu, acc, ssq):
    columns = wg.shape[1]
    half = acc.shape[1]
    for (parity, dx), segments in steps.items():
        _, pair = plane_target(scal, parity, dx)
        scaled = []
        squares = 0.0
        for core in range(2):
            blocks = [piece(kind, dy, dx) for kind, dy in segments]
            blocks = [ref.at[index, core] for ref, index in blocks]
            parts = blocks[0][half : half + 16].astype(F32)
            gain = parts[0:1] + parts[1:2] + parts[2:3]
            rows = jnp.concatenate([block[0:half] for block in blocks], axis=0).astype(F32)
            width = rows.shape[1]
            scaled.append((rows * gain).astype(BF))
            rows = rows * rows
            for j in range(width // 128):
                squares = squares + rows[:, j * 128 : (j + 1) * 128]
        left = jnp.concatenate(scaled, axis=1)
        rows = pl.ds(pl.multiple_of(pair * 2 * width, 128), 2 * width)
        gate = jnp.dot(left, wg[rows, :], preferred_element_type=F32)
        up = jnp.dot(left, wu[rows, :], preferred_element_type=F32)
        for k, (kind, dy) in enumerate(segments):
            pipe, _ = plane_target(scal, dy, dx)
            to = pipe * 2 + (kind == "b")
            here = slice(k * half, (k + 1) * half)
            acc[to, :, 0:columns] += gate[here]
            acc[to, :, columns:] += up[here]
            ssq[to] += squares[here]


def steps_of(blocks, kinds):
    steps = {}
    for parity in range(2):
        for dx in range(4):
            segments = []
            for dy in (parity, parity + 2):
                segments += [("a", dy)] if "a" in kinds and (dy, dx // 2) in blocks else []
                segments += [("b", dy)] if "b" in kinds and (dx, dy // 2) in blocks else []
            if segments:
                steps[(parity, dx)] = segments
    return steps


def on_each_core(scal, own, other, body):
    core = lax.bitwise_and(scal[0], 1)
    pl.when(core == 0)(lambda: body(own or None, other or None))
    pl.when(core == 1)(lambda: body(other or None, own or None))


def gate_up_kernel(blocks, counts, started, last, scal, *refs):
    own, refs = refs[: counts[0]], refs[counts[0] :]
    other, refs = refs[: counts[1]], refs[counts[1] :]
    (wg, wu), refs = refs[:2], refs[2:]
    acc, ssq, tok = refs[-3:]
    half = acc.shape[1]
    if started:
        for ref, before in zip((acc, ssq, tok), refs):
            ref[...] = before[...]
    else:
        for ref in (acc, ssq, tok):
            ref[...] = jnp.zeros_like(ref)

    def body(half_a, half_b):
        def piece(kind, dy, dx):
            first, second, table = (dx, dy, half_a) if kind == "a" else (dy, dx, half_b)
            array, start = blocks[(second, first // 2)]
            return table[array], start + first % 2

        kinds = ("a" if half_a else "") + ("b" if half_b else "")
        accumulate(scal, piece, steps_of(blocks, kinds), wg, wu, acc, ssq)
        if not half_a:
            return
        for (dy, _), (array, start) in blocks.items():
            pipe, _ = plane_target(scal, dy, 0)
            for at in (start, start + 1):
                for core in range(2):
                    parts = half_a[array][at, core, half : half + 16].astype(F32)
                    tok[pipe] += parts[:, 0:128] + parts[:, 128:256] + parts[:, 256:384]

    on_each_core(scal, own, other, body)
    if not last:
        return
    hidden, sums = refs[3:5]
    sums[...] = tok[scal[2]]
    columns = wg.shape[1]
    for i in range(4):
        total = jnp.sum(ssq[i], axis=1, keepdims=True)
        inverse = lax.rsqrt(total / wg.shape[0] + NORM_EPS)
        keep = inverse > 0.0
        gate = jnp.where(keep, acc[i, :, 0:columns] * inverse, 0.0)
        up = jnp.where(keep, acc[i, :, columns:] * inverse, 0.0)
        hidden[i] = (gate * sigmoid(gate) * up).astype(BF)


def gate_up(blocks, last, scal, own, other, wg, wu, *sofar):
    half = (*own, *other)[0].shape[2] - 16
    shapes = [(4, half, 2 * wg.shape[1]), (4, half, 128), (2, 16, 128)]
    if last:
        out_shape = [
            jax.ShapeDtypeStruct((4, half, wg.shape[1]), BF),
            jax.ShapeDtypeStruct((16, 128), F32),
        ]
        scratch = [pltpu.VMEM(shape, F32) for shape in shapes]
    else:
        out_shape, scratch = [jax.ShapeDtypeStruct(shape, F32) for shape in shapes], []
    values = (*own, *other, wg, wu, *sofar)
    return pl.pallas_call(
        functools.partial(
            gate_up_kernel, blocks, (len(own), len(other)), bool(sofar), last
        ),
        out_shape=out_shape,
        in_specs=[IN_SMEM] + [IN_VMEM] * len(values),
        out_specs=[IN_VMEM] * len(out_shape),
        scratch_shapes=scratch,
        compiler_params=params(28),
        name=f"gate_up_{len(blocks)}_{len(own)}_{len(other)}",
    )(scal, *values)


def down_kernel(far, steps, scal, hidden, wd, out):
    core = lax.bitwise_and(scal[0], 1)
    if far:
        core = 1 - core
    width = out.shape[3]
    for i, second in enumerate(steps):
        for first in range(4):
            dx = first + core * (second - first)
            dy = second + core * (first - second)
            pipe, pair = plane_target(scal, dy, dx)
            cols = pl.ds(pl.multiple_of(pair * 2 * width, 128), 2 * width)
            product = jnp.dot(hidden[pipe * 2 + core], wd[:, cols], preferred_element_type=F32)
            out[4 * i + first, 0] = product[:, 0:width].astype(BF)
            out[4 * i + first, 1] = product[:, width:].astype(BF)


def down(far, steps, scal, hidden, wd):
    shape = (4 * len(steps), 2, hidden.shape[1], wd.shape[1] // N_TENSOR)
    return pl.pallas_call(
        functools.partial(down_kernel, far, steps),
        out_shape=jax.ShapeDtypeStruct(shape, BF),
        in_specs=[IN_SMEM] + [IN_VMEM] * 2,
        out_specs=IN_VMEM,
        compiler_params=params(20),
        name=f"down_{'far' if far else 'near'}_{len(steps)}",
    )(scal, hidden, wd)


def add(base, *parts):
    total = base.astype(F32)
    for part in parts:
        total = total + part.astype(F32)
    return total.astype(BF)


def expert_layer(scal, extra, arrived, wg, wu, wd):
    together = lax.optimization_barrier
    half, width = arrived.shape[0] // 2, arrived.shape[1]
    block = (half + 16, width)
    keep, send = small_call(halves_kernel, [block] * 2, scal, arrived, extra)
    (both,) = small_call(pair_kernel, [(2,) + block], scal, keep, from_flip(send, 1))
    lines = [both] + [from_axis(both, True, d) for d in (1, 2, 3)]
    low0, high0 = small_call(stack_kernel, [(2, 2) + block] * 2, None, *lines)
    low1, high3 = from_axis(low0, False, 1), from_axis(high0, False, 3)
    own = (low0, high0)
    blocks = {(0, 0): (0, 0), (0, 1): (1, 0)}
    sofar = gate_up(blocks, False, scal, own, [from_flip(v, 1) for v in own], wg, wu)
    low0, high0, low1, high3, sofar = together((low0, high0, low1, high3, sofar))
    up, dn = small_call(join_kernel, [(4, 2) + block] * 2, None, low1, high0, low0, high3)
    up, dn = from_axis(up, False, 1), from_axis(dn, False, 3)
    own = (low1, high3)
    blocks = {(1, 0): (0, 0), (3, 1): (1, 0)}
    sofar = gate_up(blocks, False, scal, own, [from_flip(v, 1) for v in own], wg, wu, *sofar)
    up, dn, sofar = together((up, dn, sofar))
    own = (up, dn)
    blocks = {(2, 0): (0, 0), (1, 1): (0, 2), (3, 0): (1, 0), (2, 1): (1, 2)}
    sofar = gate_up(blocks, False, scal, own, (), wg, wu, *sofar)
    other = [from_flip(v, 1) for v in own]
    hidden, sums = gate_up(blocks, True, scal, (), other, wg, wu, *sofar)

    far = down(True, (2,), scal, hidden, wd)
    hidden, far = together((hidden, far))
    got = from_flip(far, 1)
    own = down(False, (2,), scal, hidden, wd)
    far = down(True, (0, 1, 3), scal, hidden, wd)
    low2, high2 = add(own[:2], got[:2]), add(own[2:], got[2:])
    hidden, low2, high2, far = together((hidden, low2, high2, far))
    low2, high2 = from_axis(low2, False, 3), from_axis(high2, False, 1)
    got = from_flip(far, 1)
    own = down(False, (0, 1, 3), scal, hidden, wd)
    low1, high1, low3, high3 = ((own[i : i + 2], got[i : i + 2]) for i in range(4, 12, 2))
    up = jnp.concatenate([add(*low1, low2), add(*high1)])
    dn = jnp.concatenate([add(*low3), add(*high3, high2)])
    up, dn = together((from_axis(up, False, 3), from_axis(dn, False, 1)))
    line = add(own[:4], got[:4], up, dn)
    done = add(line[0], *(from_axis(line[d], True, 4 - d) for d in (1, 2, 3)))
    core = lax.bitwise_and(scal[0], 1)
    mine = lax.dynamic_index_in_dim(done, core, 0, keepdims=False)
    other = from_flip(lax.dynamic_index_in_dim(done, 1 - core, 0, keepdims=False), 1)
    first = core == 0
    rows = [jnp.where(first, mine, other), jnp.where(first, other, mine)]
    return jnp.concatenate(rows), sums


CORE_GROUPS = [list(range(0, 16, 2)), list(range(1, 16, 2))]


def exchange(value):
    return lax.all_to_all(
        value, "tensor", split_axis=0, concat_axis=0, axis_index_groups=CORE_GROUPS
    )


def from_all(value):
    groups = [group[::-1] for group in CORE_GROUPS]
    value = jnp.broadcast_to(value[None], (8,) + value.shape)
    return lax.all_to_all(
        value, "tensor", split_axis=0, concat_axis=0, axis_index_groups=groups
    )


def product_blocks(scal, core, xt, wbuf, groups=(0, 1)):
    rows = xt.shape[1]
    for group in groups:
        slots = []
        for j in range(group * 4, group * 4 + 4):
            t = j * 2 + core
            dp = lax.bitwise_xor(lax.shift_right_logical(t, 3), scal[2])
            dz = lax.bitwise_and(lax.bitwise_and(t, 7) - scal[3] + 8, 7)
            slots.append(dp * 8 + dz)
        left = jnp.concatenate([xt[slot] for slot in slots], axis=0)
        product = jnp.dot(left, wbuf[...], preferred_element_type=F32)
        for k, slot in enumerate(slots):
            yield group * 4 + k, slot, product[k * rows : (k + 1) * rows]


def store_block(out, j, product, squares):
    rows = product.shape[0]
    out[j, 0:rows] = product.astype(BF)
    high = squares.astype(BF)
    rest = squares - high.astype(F32)
    middle = rest.astype(BF)
    low = (rest - middle.astype(F32)).astype(BF)
    empty = jnp.zeros((16, product.shape[1] - 3 * rows), BF)
    wide = [jnp.broadcast_to(v.astype(F32), (16, rows)).astype(BF) for v in (high, middle, low)]
    out[j, rows : rows + 16] = jnp.concatenate(wide + [empty], axis=1)


def proj_far_kernel(scal, gain, *refs):
    n0, u1, d1, u2, d2, u3, d3, h4, l4, s1, s2, s3 = refs[:12]
    wq, wk, wv, out, xt, sq, wbuf = refs[12:]
    half = h4.shape[0]
    n4 = jnp.concatenate([h4[...], l4[...]], axis=0)
    pieces = {0: n0, 1: u1, 7: d1, 2: u2, 6: d2, 3: u3, 5: d3}
    pieces = {i: ref[...] for i, ref in pieces.items()}
    pieces.update({4: n4, 8: s1[0], 9: s1[1], 15: s1[2], 12: s3[...]})
    pieces.update({10: s2[0], 14: s2[1], 11: s2[2], 13: s2[3]})
    ones = jnp.ones((8, n0.shape[1]), BF)
    over_features = functools.partial(
        lax.dot_general,
        dimension_numbers=(((1,), (1,)), ((), ())),
        preferred_element_type=F32,
    )
    for i, value in pieces.items():
        rows = value.astype(F32)
        xt[i] = (rows * gain[...]).astype(BF)
        squares = rows * rows
        high = squares.astype(BF)
        low = (squares - high.astype(F32)).astype(BF)
        sq[i] = over_features(ones, high) + over_features(ones, low)
    qw = wq.shape[1]
    head = pl.ds(pl.multiple_of(scal[4] * HD, HD), HD)
    wbuf[:, 0:qw] = wq[...]
    wbuf[:, qw : qw + HD] = wk[:, head]
    wbuf[:, qw + HD :] = wv[:, head]
    core = 1 - lax.bitwise_and(scal[0], 1)
    for j, slot, product in product_blocks(scal, core, xt, wbuf, (0,)):
        store_block(out, j, product, sq[slot][0:1])


def proj_far_rest_kernel(scal, xt, sq, wbuf, out):
    core = 1 - lax.bitwise_and(scal[0], 1)
    for j, slot, product in product_blocks(scal, core, xt, wbuf, (1,)):
        store_block(out, j - 4, product, sq[slot][0:1])


def proj_own_kernel(scal, xt, wbuf, out):
    core = lax.bitwise_and(scal[0], 1)
    for j, _, product in product_blocks(scal, core, xt, wbuf):
        out[j] = product


def proj_near_kernel(scal, got0, got1, own, sq, out):
    rows = own.shape[1]
    core = lax.bitwise_and(scal[0], 1)
    for j in range(8):
        got = (got0, got1)[j // 4]
        t = j * 2 + core
        dp = lax.bitwise_xor(lax.shift_right_logical(t, 3), scal[2])
        dz = lax.bitwise_and(lax.bitwise_and(t, 7) - scal[3] + 8, 7)
        parts = got[j % 4, rows : rows + 16].astype(F32)
        squares = sq[dp * 8 + dz][0:1]
        for k in (2, 1, 0):
            squares = squares + parts[0:1, k * rows : (k + 1) * rows]
        store_block(out, j, own[j] + got[j % 4, 0:rows].astype(F32), squares)


def projections(scal, gain, tokens, wq, wk, wv):
    rows, width = tokens[0].shape
    columns = wq.shape[1] + 2 * HD
    sums = jax.ShapeDtypeStruct((8, rows + 16, columns), BF)
    half = jax.ShapeDtypeStruct((4, rows + 16, columns), BF)
    far, xt, sq, wbuf = pl.pallas_call(
        proj_far_kernel,
        out_shape=[
            half,
            jax.ShapeDtypeStruct((16, rows, width), BF),
            jax.ShapeDtypeStruct((16, 8, rows), F32),
            jax.ShapeDtypeStruct((width, columns), BF),
        ],
        in_specs=[IN_SMEM] + [IN_VMEM] * 16,
        out_specs=[IN_VMEM] * 4,
        compiler_params=params(20),
        name="proj_far",
    )(scal, gain, *tokens, wq, wk, wv)
    far, xt, sq, wbuf = lax.optimization_barrier((far, xt, sq, wbuf))
    got0 = from_flip(far, 1)

    def call(kernel, out_shape, *values):
        return pl.pallas_call(
            kernel,
            out_shape=out_shape,
            in_specs=[IN_SMEM] + [IN_VMEM] * len(values),
            out_specs=IN_VMEM,
            compiler_params=params(20),
            name=kernel.__name__,
        )(scal, *values)

    rest = call(proj_far_rest_kernel, half, xt, sq, wbuf)
    rest, xt, wbuf = lax.optimization_barrier((rest, xt, wbuf))
    got1 = from_flip(rest, 1)
    own = call(proj_own_kernel, jax.ShapeDtypeStruct((8, rows, columns), F32), xt, wbuf)
    near = call(proj_near_kernel, sums, got0, got1, own, sq)
    total = jnp.sum(exchange(near).astype(F32), axis=0)
    parts = total[rows, : 3 * rows].reshape(3, rows)
    return total[:rows], parts[0] + (parts[1] + parts[2])


def attend_kernel(far, scal, q, kv, *refs):
    rows = q.shape[0]
    heads = q.shape[1] // HD
    own = scal[0]
    core = lax.bitwise_and(own, 1)
    core = 1 - core if far else core
    keys, values, places = [], [], []
    for j in range(8):
        block = kv[j]
        keys.append(block[:, :HD])
        values.append(block[:, HD:])
        base = (14 - 2 * j + core) * rows
        places.append(lax.broadcasted_iota(jnp.int32, (rows, rows), 1) + base)
    keys = jnp.concatenate(keys, axis=0)
    values = jnp.concatenate(values, axis=0)
    places = jnp.concatenate(places, axis=1)
    mine = lax.broadcasted_iota(jnp.int32, places.shape, 0) + own * rows
    allowed = places <= mine
    for h in range(heads):
        here = slice(h * HD, (h + 1) * HD)
        scores = lax.dot_general(
            q[:, here], keys, (((1,), (1,)), ((), ())), preferred_element_type=F32
        ) * (1.0 / math.sqrt(HD))
        scores = jnp.where(allowed, scores, -1e30)
        best = jnp.max(scores, axis=1, keepdims=True)
        if far:
            before, bests, totals, out = refs
            old = bests[:, here][:, 0:1]
            best = jnp.maximum(best, old)
        weights = jnp.where(allowed, jnp.exp(scores - best), 0.0)
        total = jnp.sum(weights, axis=1, keepdims=True)
        mixed = jnp.dot(weights.astype(BF), values, preferred_element_type=F32)
        if far:
            shrink = jnp.exp(old - best)
            total = total + totals[:, here][:, 0:1] * shrink
            out[:, here] = ((mixed + before[:, here] * shrink) / total).astype(BF)
        else:
            mixed_out, bests, totals = refs
            mixed_out[:, here] = mixed
            bests[:, here] = jnp.broadcast_to(best, mixed.shape)
            totals[:, here] = jnp.broadcast_to(total, mixed.shape)


def attend(far, scal, q, kv, *sofar):
    shapes = [jax.ShapeDtypeStruct(q.shape, BF)] if far else [jax.ShapeDtypeStruct(q.shape, F32)] * 3
    return pl.pallas_call(
        functools.partial(attend_kernel, far),
        out_shape=shapes,
        in_specs=[IN_SMEM] + [IN_VMEM] * (2 + len(sofar)),
        out_specs=[IN_VMEM] * len(shapes),
        compiler_params=params(24),
        name="attend_far" if far else "attend_near",
    )(scal, q, kv, *sofar)


def gather_tokens(own):
    half = own.shape[0] // 2
    u1, d1 = from_z(own, 1), from_z(own, 7)
    s1 = from_pipe(jnp.stack([own, u1, d1]))
    u2, d2 = from_z(u1, 1), from_z(d1, 7)
    u3, d3 = from_z(u2, 1), from_z(d2, 7)
    u3, d3, s1 = lax.optimization_barrier((u3, d3, s1))
    s2 = from_pipe(jnp.stack([u2, d2, u3, d3]))
    h4, l4 = from_z(u3[:half], 1), from_z(d3[half:], 7)
    s3 = from_pipe(jnp.concatenate([h4, l4]))
    return (own, u1, d1, u2, d2, u3, d3, h4, l4, s1, s2, s3)


def on_device(
    stream,
    norm_gain,
    attn_gain,
    router,
    expert_ids,
    expert_slots,
    w_gate,
    w_up,
    w_down,
    w_query,
    w_key,
    w_value,
):
    token_rows, width = stream.shape
    features = width * N_TENSOR
    experts = router.shape[1]
    query_width = w_query.shape[1]
    heads_here = query_width // HD
    t = lax.axis_index("tensor")
    pipe = lax.axis_index("pipe")
    z = lax.axis_index("expert")
    kv_head = (pipe * 8 + z) * heads_here // (QH // KVH)
    yy = pipe * 2 + (t // 2) % 2
    scal = jnp.stack([t, yy, pipe, z, kv_head]).astype(jnp.int32)

    outgoing, extra = prepare(
        stream, norm_gain.reshape(1, width), router.T, expert_ids.T, expert_slots.T
    )
    scal, outgoing, extra = lax.optimization_barrier((scal, outgoing, extra))
    arrived = lax.all_to_all(outgoing, "expert", split_axis=0, concat_axis=0, tiled=True)
    expert_out, sums = expert_layer(scal, extra, arrived, w_gate[0], w_up[0], w_down[0])
    returned = lax.all_to_all(
        expert_out.reshape(experts, CAP, width),
        "expert",
        split_axis=0,
        concat_axis=0,
        axis_index_groups=[list(range(experts))[::-1]],
    ).reshape(experts * CAP, width)

    inverse = lax.rsqrt(sums[3] / features + NORM_EPS)
    first_share = jax.nn.sigmoid(inverse * sums[4])
    second_share = 1.0 - first_share

    slot_total = experts * CAP
    place = (experts - 1 - expert_ids) * CAP + expert_slots
    target = jnp.where(expert_slots >= 0, place, slot_total)
    slots = jnp.arange(slot_total, dtype=jnp.int32)
    stream_f = stream.astype(F32)
    wanted = jnp.concatenate([target[:, 0], target[:, 1]])
    picks = (wanted[:, None] == slots[None]).astype(BF)
    picked = jnp.dot(picks, returned, preferred_element_type=F32)
    moe_sum = (
        first_share[:, None] * picked[:token_rows] + second_share[:, None] * picked[token_rows:]
    )
    new_stream = (stream_f + moe_sum).astype(BF)

    tokens = gather_tokens(new_stream)
    own_proj, squares_two = projections(
        scal, attn_gain.reshape(1, width), tokens, w_query, w_key, w_value
    )
    inverse_two = lax.rsqrt(squares_two / features + NORM_EPS)[:, None]
    own_proj = jnp.where(inverse_two > 0.0, own_proj * inverse_two, 0.0).astype(BF)
    queries = own_proj[:, :query_width]
    kv = own_proj[:, query_width:]
    kv = from_all(kv)
    other = from_flip(kv, 1)
    (attended,) = attend(True, scal, queries, other, *attend(False, scal, queries, kv))
    return (new_stream, attended)


def solution(mesh):
    in_specs = (
        P(("pipe", "expert"), "tensor"),
        P("tensor"),
        P("tensor"),
        P("tensor", None),
        P(("pipe", "expert"), None),
        P(("pipe", "expert"), None),
        P("expert", None, ("pipe", "tensor")),
        P("expert", None, ("pipe", "tensor")),
        P("expert", ("pipe", "tensor"), None),
        P("tensor", ("pipe", "expert")),
        P("tensor", None),
        P("tensor", None),
    )
    out_specs = (P(("pipe", "expert"), "tensor"), P("tensor", ("pipe", "expert")))
    return jax.shard_map(
        on_device, mesh=mesh, in_specs=in_specs, out_specs=out_specs, check_vma=False
    )
```
